256 devices in a mesh: gx: 8 (over x, y_lo), gy: 32 (over z, y_hi, core).
Axes of the slice: x: 4, y: 4 (y_hi: 2, y_lo: 2; y = y_hi * 2 + y_lo), z: 8, core: 2. Of those that a mesh axis runs over, the one named last changes fastest.
Arguments:
- frames: bfloat16 [65536, 1280], P(('gx', 'gy')), may hold values from -6 to 6
- lengths: int32 [256], replicated, may hold values from 1 to 256, 32768 in all
- matchings: int32 [2, 256], replicated, may hold values from 0 to 255, as said below
- wqkv: bfloat16 [2, 1280, 3840], P(None, 'gy'), may hold values from -1 to 1
- wout: bfloat16 [1, 1280, 1280], P(None, 'gy'), may hold values from -0.15625 to 0.15625
Outputs:
- stream: bfloat16 [65536, 1280], P(('gx', 'gy'))
- context: bfloat16 [65536, 1280], P(('gx', 'gy'))
The draws below stay inside these ranges and needn't reach their ends.
Inputs may be any that keep to these rules, and one draw needn't show every extreme that they name: `matchings`: each row pairs the blocks: the partner of a block's partner is the block itself, and no block is its own partner. The lengths sum to 32768 and some block has all 256 frames valid.
All inputs are finite; a program needn't handle non-finite values.
Results may differ from the reference program's by a relative error of at most 0.029.
The reference program's roundings to bfloat16 on the way count: a program that leaves them out, or rounds other values in their place, can miss the bound.
Values may be sent and summed in bfloat16 or wider, within the bound.
No kernel may reach another device: no remote copies, remote signals or barrier semaphores. Data moves between devices by JAX's collectives and lax.ppermute only.
A program may use at most 128 MiB of HBM per device.

```python
import math
import jax
import jax.numpy as jnp
import numpy as np
from jax import lax

HEAD_DIM = 64
D = 1280
LAYERS = 2
HALO = 128
BLK = 256
BLOCKS = 256
FRAMES = 65536


def draw_frames(key, part):
    key = jax.random.fold_in(key, 11)
    base = jnp.clip(jax.random.normal(key, (FRAMES, D), jnp.float32), -6.0, 6.0)
    return base.astype(jnp.bfloat16)


def draw_matchings(key, part):
    key = jax.random.fold_in(key, 5)
    layers_out = []
    for layer in range(LAYERS):
        order = jax.random.permutation(jax.random.fold_in(key, layer), BLOCKS).astype(jnp.int32)
        swapped = order.reshape(-1, 2)[:, ::-1].reshape(-1)
        partner = jnp.zeros((BLOCKS,), jnp.int32).at[order].set(swapped)
        layers_out.append(partner)
    return jnp.stack(layers_out)


def draw_wqkv(key, part):
    key = jax.random.fold_in(key, 7)
    shape = (LAYERS, D, 3 * D)
    base = jnp.clip(jax.random.normal(key, shape, jnp.float32), -6.0, 6.0) / D ** 0.5
    return base.astype(jnp.bfloat16)


def steps_of(key, extent, split, low, top_value):
    gain = 1.0
    for dim, blocks in split:
        draws = jax.random.uniform(jax.random.fold_in(jax.random.fold_in(key, 6), dim), (blocks,), jnp.float32, low / len(split), top_value / len(split))
        gain = gain * jnp.repeat(jnp.exp(draws), extent[dim] // blocks).reshape((-1,) + (1,) * (len(extent) - 1 - dim))
    return gain


def profile(amount, total, most, lean):
    portions = [(1 << 20) // math.isqrt(grade ** lean) + 1 for grade in range(2, amount + 1)]
    spare, given = total - most - (amount - 1), [1] * (amount - 1)
    while spare > 0:
        candidates = [i for i in range(amount - 1) if given[i] < most]
        whole, left = sum([portions[i] for i in candidates]), spare
        for i in candidates:
            addition = min(most - given[i], max(1, left * portions[i] // whole), spare)
            given[i] = given[i] + addition
            spare = spare - addition
    return np.array([most] + given)


def ragged_sizes(own_key, count, total, most, lean):
    if count == 2:
        one = jax.random.randint(own_key, (), max(1, total - most), min(most, total - 1) + 1)
        return jnp.stack([one, total - one])
    tallies = jnp.asarray(profile(count, total, most, lean), jnp.int32)
    couples = (count - 1) // 2
    giver, receiver = tallies[1:1 + 2 * couples:2], tallies[2:2 + 2 * couples:2]
    margin = jnp.minimum(giver - 1, most - receiver)
    passed = jax.random.randint(jax.random.fold_in(own_key, 1), (couples,), 0, 1 << 20) % (margin + 1)
    tallies = tallies.at[1:1 + 2 * couples:2].set(giver - passed).at[2:2 + 2 * couples:2].set(receiver + passed)
    return tallies[jax.random.permutation(jax.random.fold_in(own_key, 2), count)]


def gaussian(own_key, dims, scale, most, cuts=(), held_as=jnp.bfloat16):
    entries = jax.random.normal(own_key, dims, jnp.float32) * scale
    if len(cuts) > 0:
        entries = steps_of(own_key, dims, cuts, -0.22, 0.18) * entries
    return jnp.clip(entries, min=-most, max=most).astype(held_as)


def setup_inputs(seed: int = 0) -> dict:
    key_of = jax.random.split(jax.random.key(seed), 6)
    frames = draw_frames(jax.random.fold_in(key_of[5], 71), 0)
    lengths = ragged_sizes(key_of[1], BLOCKS, BLOCKS * BLK // 2, BLK, 2).astype(jnp.int32)
    matchings = draw_matchings(jax.random.fold_in(key_of[5], 71), 0)
    wqkv = draw_wqkv(jax.random.fold_in(key_of[5], 71), 0)
    wout = gaussian(key_of[4], (LAYERS - 1, D, D), D ** -0.5, 0.15625, ((1, 32),))
    return dict(frames=frames, lengths=lengths, matchings=matchings, wqkv=wqkv, wout=wout)


def normalize(rows):
    values = rows.astype(jnp.float32)
    mean = lax.optimization_barrier(jnp.mean(values, axis=-1, keepdims=True))
    centred = values - mean
    variance = lax.optimization_barrier(jnp.mean(centred * centred, axis=-1, keepdims=True))
    return (centred * lax.rsqrt(variance + 1e-05)).astype(jnp.bfloat16)

def attend(query, keys, values, valid):
    count = keys.shape[0]
    rows, width = query.shape
    heads = width // HEAD_DIM
    q_heads = query.reshape(rows, heads, HEAD_DIM).astype(jnp.float32)
    k_heads = keys.reshape(count, heads, HEAD_DIM).astype(jnp.float32)
    v_heads = values.reshape(count, heads, HEAD_DIM).astype(jnp.float32)
    scores = jnp.einsum('qhd,khd->hqk', q_heads, k_heads) * 0.125
    scores = jnp.where(valid[None, None, :], scores, jnp.float32(-1e+30))
    top = lax.optimization_barrier(jnp.max(scores, axis=-1, keepdims=True))
    expo = jnp.exp(scores - top)
    total = lax.optimization_barrier(jnp.sum(expo, axis=-1))
    probs = expo.astype(jnp.bfloat16).astype(jnp.float32)
    mixed = jnp.einsum('hqk,khd->qhd', probs, v_heads)
    mixed = mixed / jnp.transpose(total)[:, :, None]
    return mixed.reshape(rows, width).astype(jnp.bfloat16)

def reference(frames, lengths, matchings, wqkv, wout):
    blocks = lengths.shape[0]
    blk = frames.shape[0] // blocks
    width = frames.shape[1]
    hidden = frames
    context = frames
    for layer in range(LAYERS):
        normed = normalize(hidden)
        qkv = jnp.dot(normed, wqkv[layer], preferred_element_type=jnp.float32).astype(jnp.bfloat16)
        query_all = qkv[:, :width]
        kv_all = qkv[:, width:]
        partner = matchings[layer]

        def one_block(index):
            own = lax.dynamic_slice_in_dim(kv_all, (index * blk).astype(jnp.int32), blk, 0)
            other_id = partner[index].astype(jnp.int32)
            other = lax.dynamic_slice_in_dim(kv_all, (other_id * blk).astype(jnp.int32), blk, 0)
            before = jnp.maximum(index - 1, 0).astype(jnp.int32)
            len_before = lengths[before]
            tail_start = jnp.maximum(len_before - HALO, 0).astype(jnp.int32)
            tail = lax.dynamic_slice_in_dim(kv_all, (before * blk + tail_start).astype(jnp.int32), HALO, 0)
            row_ids = jnp.arange(blk, dtype=jnp.int32)
            tail_ids = jnp.arange(HALO, dtype=jnp.int32)
            valid = jnp.concatenate([row_ids < lengths[index], row_ids < lengths[other_id], (tail_ids < jnp.minimum(len_before, HALO)) & (index > 0)])
            joined = jnp.concatenate([own, other, tail], axis=0)
            query = lax.dynamic_slice_in_dim(query_all, (index * blk).astype(jnp.int32), blk, 0)
            return attend(query, joined[:, :width], joined[:, width:], valid)
        context = lax.map(one_block, jnp.arange(blocks, dtype=jnp.int32)).reshape(-1, width)
        if layer < LAYERS - 1:
            update = jnp.dot(context, wout[layer], preferred_element_type=jnp.float32)
            hidden = (hidden.astype(jnp.float32) + update).astype(jnp.bfloat16)
    return (hidden, context)
```

```python
import functools
import math

import jax
import jax.numpy as jnp
from jax import lax
from jax.experimental import pallas as pl
from jax.experimental.pallas import tpu as pltpu
from jax.sharding import PartitionSpec as P

ALL = ("gx", "gy")
HEAD_DIM = 64
HALO = 128
BLK = 256
D = 1280
HALF = D // 2
PAIR = 2 * HEAD_DIM
STEPS = D // (2 * PAIR)
SCALE_LOG2 = 0.125 * math.log2(math.e)


def flat_pairs(move):
    pairs = []
    for gx in range(8):
        for gy in range(32):
            x, y_lo, z, y_hi, core = move(gx // 2, gx % 2, gy // 4, (gy // 2) % 2, gy % 2)
            pairs.append((gx * 32 + gy, (x % 4 * 2 + y_lo) * 32 + z % 8 * 4 + y_hi * 2 + core))
    return pairs


CORE_SWAP = flat_pairs(lambda x, l, z, h, c: (x, l, z, h, 1 - c))
CROSS_SWAP = flat_pairs(lambda x, l, z, h, c: (x, 1 - l, z, 1 - h, c))
X_UP = flat_pairs(lambda x, l, z, h, c: (x + 1, l, z, h, c))
X_DOWN = flat_pairs(lambda x, l, z, h, c: (x - 1, l, z, h, c))
Z_GROUPS = [[z * 4 + k for z in range(8)] for k in range(4)]
X_GROUPS = [[x * 2 + k for x in range(4)] for k in range(2)]


def lookup(table, index):
    return jnp.sum(jnp.where(jnp.arange(table.shape[0], dtype=jnp.int32) == index, table, 0))


def lookup_all(table, index):
    ids = jnp.arange(table.shape[0], dtype=jnp.int32)
    return jnp.sum(jnp.where(ids[None, :] == index[:, None], table[None, :], 0), axis=1)


def standardized(rows):
    values = rows.astype(jnp.float32)
    mean = jnp.mean(values, axis=-1, keepdims=True)
    centred = values - mean
    variance = jnp.mean(centred * centred, axis=-1, keepdims=True)
    return (centred * lax.rsqrt(variance + 1e-05)).astype(jnp.bfloat16)


def layer_kernel(with_out, scal, *refs):
    own, other, tail, q0, k0, v0, q1, k1, v1 = refs[:9]
    rest = refs[9:]
    if with_out:
        wo0, wo1 = rest[:2]
        rest = rest[2:]
    out, normed, ctx = rest
    step = pl.program_id(0)

    @pl.when(step == 0)
    def _():
        normed[pl.ds(0, BLK), :] = standardized(own[...].reshape(BLK, D))
        normed[pl.ds(BLK, BLK), :] = standardized(other[...].reshape(BLK, D))
        normed[pl.ds(2 * BLK, HALO), :] = standardized(tail[...].reshape(HALO, D))

    count = 2 * BLK + HALO
    row = lax.broadcasted_iota(jnp.int32, (count, PAIR), 0)
    lane_k = lax.broadcasted_iota(jnp.int32, (count, PAIR), 1)
    lane_q = lax.broadcasted_iota(jnp.int32, (BLK, PAIR), 1)
    limit = jnp.where(
        row < BLK,
        scal[1],
        jnp.where(row < 2 * BLK, scal[2] + BLK, scal[3] + 2 * BLK),
    )
    bias = jnp.where(row < limit, 0.0, -1e30).astype(jnp.float32)

    x_all = normed[...]
    dot = functools.partial(jnp.dot, preferred_element_type=jnp.float32)
    q = dot(normed[pl.ds(0, BLK), :], jnp.concatenate([q0[0], q1[0]], axis=1))
    k = dot(x_all, jnp.concatenate([k0[0], k1[0]], axis=1))
    v = dot(x_all, jnp.concatenate([v0[0], v1[0]], axis=1)).astype(jnp.bfloat16)
    core = scal[0]
    for pair in range(2):
        lanes = slice(pair * PAIR, (pair + 1) * PAIR)
        q_pair, k_pair, v_pair = q[:, lanes], k[:, lanes], v[:, lanes]
        parts = []
        for head in range(2):
            mine_q = (lane_q < HEAD_DIM) if head == 0 else (lane_q >= HEAD_DIM)
            spare = HEAD_DIM if head == 0 else 0
            q_head = jnp.where(
                mine_q, q_pair, jnp.where(lane_q == spare, 1.0, 0.0)
            ).astype(jnp.bfloat16)
            k_head = jnp.where(lane_k == spare, bias, k_pair).astype(jnp.bfloat16)
            scores = lax.dot_general(
                q_head, k_head, (((1,), (1,)), ((), ())), preferred_element_type=jnp.float32
            )
            top = jnp.max(scores, axis=-1, keepdims=True)
            expo = jnp.exp2((scores - top) * SCALE_LOG2)
            total = jnp.sum(expo, axis=-1, keepdims=True)
            mixed = dot(expo.astype(jnp.bfloat16), v_pair)
            parts.append(mixed / total)
        both = jnp.where(lane_q < HEAD_DIM, parts[0], parts[1]).astype(jnp.bfloat16)
        half = core if pair == 0 else 1 - core
        place = pl.multiple_of((half * STEPS + step) * PAIR, PAIR)
        ctx[:, pl.ds(place, PAIR)] = both

    @pl.when(step == STEPS - 1)
    def _():
        if with_out:
            context = ctx[...]
            for half, weight in ((core, wo0), (1 - core, wo1)):
                place = pl.ds(pl.multiple_of(half * HALF, 128), HALF)
                update = dot(context, weight[0])
                here = own[..., place].reshape(BLK, HALF).astype(jnp.float32)
                out[:, place] = (here + update).astype(jnp.bfloat16)
        else:
            out[...] = ctx[...]


def layer(scal, own, other, tail, mine, yours, with_out):
    tiles = mine.shape[2] // PAIR

    def whole(pair):
        array, index = pair
        if index is None:
            return pl.BlockSpec(array.shape, lambda i, s: (0,) * array.ndim)
        at, size = index
        return pl.BlockSpec((size, HALO, D), lambda i, s: (at // size, 0, 0))

    def tile(first):
        return pl.BlockSpec(
            (1, D, PAIR), lambda i, s: ((first + i) // tiles, 0, (first + i) % tiles)
        )

    weights = [tile(0), tile(STEPS), tile(2 * STEPS)] * 2
    operands = [mine] * 3 + [yours] * 3
    if with_out:
        weights += [pl.BlockSpec((1, D, HALF), lambda i, s: (3, 0, 0))] * 2
        operands += [mine, yours]
    return pl.pallas_call(
        functools.partial(layer_kernel, with_out),
        grid_spec=pltpu.PrefetchScalarGridSpec(
            num_scalar_prefetch=1,
            grid=(STEPS,),
            in_specs=[whole(own), whole(other), whole(tail)] + weights,
            out_specs=pl.BlockSpec((BLK, D), lambda i, s: (0, 0)),
            scratch_shapes=[
                pltpu.VMEM((2 * BLK + HALO, D), jnp.bfloat16),
                pltpu.VMEM((BLK, D), jnp.bfloat16),
            ],
        ),
        out_shape=jax.ShapeDtypeStruct((BLK, D), jnp.bfloat16),
        compiler_params=pltpu.CompilerParams(
            dimension_semantics=("arbitrary",), vmem_limit_bytes=48 * 1024 * 1024
        ),
        cost_estimate=pl.CostEstimate(
            flops=8 * 10**9, bytes_accessed=14 * 10**6, transcendentals=4 * 10**6
        ),
    )(scal, own[0], other[0], tail[0], *operands)


def gather_weights(wqkv, wout, x, core, y_hi):
    first = jnp.concatenate([wqkv[0], wout[0]], axis=1)
    second = wqkv[1].reshape(-1, 3, 2, HALF)

    def column_block(half):
        part_0 = lax.dynamic_slice_in_dim(first, (x * 2 + half) * HALF, HALF, 1)
        part_1 = lax.dynamic_index_in_dim(second, half, 2, keepdims=False).reshape(-1, 3 * HALF)
        part_1 = jnp.pad(part_1, ((0, 0), (0, 128)))
        return jnp.concatenate(
            [part_0, lax.dynamic_slice_in_dim(part_1, x * 512, 512, 1)], axis=1
        )

    def in_order(first_place, mine, yours):
        return jnp.where(
            first_place,
            jnp.concatenate([mine, yours], axis=0),
            jnp.concatenate([yours, mine], axis=0),
        )

    chip = in_order(
        core == 0, column_block(core), lax.ppermute(column_block(1 - core), ALL, CORE_SWAP)
    )
    plane = in_order(y_hi == 0, chip, lax.ppermute(chip, ALL, CROSS_SWAP))
    columns = lax.all_gather(plane, "gy", axis=0, tiled=True, axis_index_groups=Z_GROUPS)
    mine_0 = lax.all_gather(columns[:, :HALF], "gx", axis=0, axis_index_groups=X_GROUPS)
    mine_1 = lax.all_gather(columns[:, HALF:], "gx", axis=0, axis_index_groups=X_GROUPS)
    yours_0 = lax.ppermute(mine_0, ALL, CORE_SWAP)
    yours_1 = lax.ppermute(mine_1, ALL, CORE_SWAP)
    return mine_0, yours_0, mine_1, yours_1


def local(frames, lengths, matchings, wqkv, wout):
    gx, gy = lax.axis_index("gx"), lax.axis_index("gy")
    here = gx * 32 + gy
    core, y_hi, x = gy % 2, (gy // 2) % 2, gx // 2
    mine_0, yours_0, mine_1, yours_1 = gather_weights(wqkv, wout, x, core, y_hi)

    spread_in = frames.reshape(2, HALO, 2, HALF).transpose(2, 1, 0, 3).reshape(256, 2, HALF)
    spread = lax.all_to_all(spread_in, ALL, 0, 0, tiled=True).reshape(512, HALF)

    blocks = jnp.arange(256, dtype=jnp.int32)
    partner_0, partner_1 = matchings[0], matchings[1]
    second = lookup_all(partner_0, partner_1)
    before = jnp.maximum(blocks - 1, 0)
    before_1 = jnp.maximum(partner_1 - 1, 0)
    m = here % HALO
    start = jnp.maximum(lengths - HALO, 0)
    high = (m < start).astype(jnp.int32)
    wanted = jnp.stack(
        [
            2 * partner_0,
            2 * partner_0 + 1,
            2 * partner_1,
            2 * partner_1 + 1,
            2 * second,
            2 * second + 1,
            2 * before_1 + lookup_all(high, before_1),
            2 * before + lookup_all(high, before),
        ],
        axis=1,
    ).reshape(-1)
    chosen = (wanted[:, None] == jnp.arange(512, dtype=jnp.int32)[None, :]).astype(jnp.bfloat16)
    routed = jnp.dot(chosen, spread, preferred_element_type=jnp.float32).astype(jnp.bfloat16)
    collected = lax.all_to_all(routed.reshape(256, 8, HALF), ALL, 0, 0, tiled=True)
    rows = collected.reshape(2, HALO, 8, HALF).transpose(2, 1, 0, 3).reshape(8, HALO, D)

    block_0, block_1 = lookup(partner_0, here), lookup(partner_1, here)
    block_2 = lookup(partner_0, block_1)
    len_here = lookup(lengths, here)
    len_1 = lookup(lengths, block_1)

    def tail_count(block):
        known = jnp.minimum(lookup(lengths, jnp.maximum(block - 1, 0)), HALO)
        return jnp.where(block > 0, known, 0)

    def scalars(*values):
        return jnp.stack([v.astype(jnp.int32) for v in (core, *values)])

    hidden = layer(
        scalars(len_here, lookup(lengths, block_0), tail_count(here)),
        (frames, None),
        (rows, (0, 2)),
        (rows, (7, 1)),
        mine_0,
        yours_0,
        True,
    )
    own_tail = lax.dynamic_slice_in_dim(hidden, jnp.maximum(len_here - HALO, 0), HALO, 0)
    tail_1 = lax.ppermute(own_tail, ALL, [(i, i + 1) for i in range(255)])
    hidden_1 = layer(
        scalars(len_1, lookup(lengths, block_2), tail_count(block_1)),
        (rows, (2, 2)),
        (rows, (4, 2)),
        (rows, (6, 1)),
        mine_0,
        yours_0,
        True,
    )
    context = layer(
        scalars(len_here, len_1, tail_count(here)),
        (hidden, None),
        (hidden_1, None),
        (tail_1, None),
        mine_1,
        yours_1,
        False,
    )
    return hidden, context


def solution(mesh):
    rows = P(ALL, None)
    return jax.shard_map(
        local,
        mesh=mesh,
        in_specs=(rows, P(), P(), P(None, "gy", None), P(None, "gy", None)),
        out_specs=(rows, rows),
        check_vma=False,
    )
```

```python
import functools
import math

import jax
import jax.numpy as jnp
from jax import lax
from jax.experimental import pallas as pl
from jax.experimental.pallas import tpu as pltpu
from jax.sharding import PartitionSpec as P

ALL = ("gx", "gy")
HEAD_DIM = 64
HALO = 128
BLK = 256
D = 1280
HALF = D // 2
PAIR = 2 * HEAD_DIM
STEPS = D // (2 * PAIR)
PIECES = 5
SCALE_LOG2 = 0.125 * math.log2(math.e)


def flat_pairs(move):
    pairs = []
    for gx in range(8):
        for gy in range(32):
            x, y_lo, z, y_hi, core = move(gx // 2, gx % 2, gy // 4, (gy // 2) % 2, gy % 2)
            pairs.append((gx * 32 + gy, (x % 4 * 2 + y_lo) * 32 + z % 8 * 4 + y_hi * 2 + core))
    return pairs


CORE_SWAP = flat_pairs(lambda x, l, z, h, c: (x, l, z, h, 1 - c))
CROSS_SWAP = flat_pairs(lambda x, l, z, h, c: (x, 1 - l, z, 1 - h, c))
FAR_SWAP = flat_pairs(lambda x, l, z, h, c: (x, 1 - l, z, 1 - h, 1 - c))
X_UP = flat_pairs(lambda x, l, z, h, c: (x + 1, l, z, h, c))
X_DOWN = flat_pairs(lambda x, l, z, h, c: (x - 1, l, z, h, c))
Z_GROUPS = [[z * 4 + k for z in range(8)] for k in range(4)]


def lookup(table, index):
    return jnp.sum(jnp.where(jnp.arange(table.shape[0], dtype=jnp.int32) == index, table, 0))


def lookup_all(table, index):
    ids = jnp.arange(table.shape[0], dtype=jnp.int32)
    return jnp.sum(jnp.where(ids[None, :] == index[:, None], table[None, :], 0), axis=1)


def standardized(rows):
    values = rows.astype(jnp.float32)
    mean = jnp.mean(values, axis=-1, keepdims=True)
    centred = values - mean
    variance = jnp.mean(centred * centred, axis=-1, keepdims=True)
    return (centred * lax.rsqrt(variance + 1e-05)).astype(jnp.bfloat16)


def layer_kernel(first_block, with_out, scal, lengths, matchings, *refs):
    tiles = refs[0].shape[1] // PAIR
    sources, refs = (refs[:PIECES], refs[PIECES : 2 * PIECES]), refs[2 * PIECES :]
    if first_block:
        own, refs = refs[0], refs[1:]
    if with_out:
        collected, out, normed, ctx, weights, weight_sems, out_weights, out_sems, spare = refs
    else:
        other, tail, out, normed, ctx, weights, weight_sems = refs
    step = pl.program_id(0)
    here, core, x = scal[0], scal[1], scal[2]
    block = here if first_block else matchings[1, here]
    partner = matchings[0 if with_out else 1, block]
    known = jnp.minimum(lengths[jnp.maximum(block - 1, 0)], HALO)
    known = jnp.where(block > 0, known, 0)

    def slot_half(at, half):
        rows = pl.ds(half * 1024 + at, HALO, stride=8)
        return jnp.concatenate([spare[i, rows, :] for i in range(HALF // 128)], axis=1)

    def start_tile(half, x_here, index, target, width, sem):
        place = (index // tiles - x_here) % 4
        columns = pl.ds(index % tiles * PAIR, width)
        side = sources[half]
        if place == 2:
            rows = D // 2
            for part in range(2):
                pltpu.make_async_copy(
                    side[2 + part].at[:, columns], target.at[pl.ds(part * rows, rows)], sem
                ).start()
        else:
            pltpu.make_async_copy(side[(0, 1, 2, 4)[place]].at[:, columns], target, sem).start()

    @pl.when(step == 0)
    def _():
        for x_here in range(4):

            @pl.when(x == x_here)
            def _():
                for at in range(STEPS):
                    for kind in range(3):
                        for half in range(2):
                            start_tile(
                                half,
                                x_here,
                                kind * STEPS + at,
                                weights.at[at, kind, :, pl.ds(half * PAIR, PAIR)],
                                PAIR,
                                weight_sems.at[at, kind, half],
                            )
                if with_out:
                    for half in range(2):
                        start_tile(
                            half, x_here, 3 * STEPS, out_weights.at[half], HALF, out_sems.at[half]
                        )

        if with_out:
            for lane_tile in range(HALF // 128):
                lanes = pl.ds(lane_tile * 128, 128)
                spare[lane_tile] = collected[:, lanes].astype(jnp.float32)

            def slot(at):
                return jnp.concatenate([slot_half(at, 0), slot_half(at, 1)], axis=1)

            slots = (0, 1, 7) if first_block else (2, 3, 4, 5, 6)
            if first_block:
                normed[pl.ds(0, BLK), :] = standardized(own[...])
            base = BLK if first_block else 0
            for order, at in enumerate(slots):
                normed[pl.ds(base + order * HALO, HALO), :] = standardized(slot(at))
        else:
            normed[pl.ds(0, BLK), :] = standardized(own[...])
            normed[pl.ds(BLK, BLK), :] = standardized(other[...])
            normed[pl.ds(2 * BLK, HALO), :] = standardized(tail[...])

    for kind in range(3):
        for half in range(2):
            target = weights.at[step, kind, :, pl.ds(half * PAIR, PAIR)]
            pltpu.make_async_copy(target, target, weight_sems.at[step, kind, half]).wait()

    count = 2 * BLK + HALO
    row = lax.broadcasted_iota(jnp.int32, (count, PAIR), 0)
    lane_k = lax.broadcasted_iota(jnp.int32, (count, PAIR), 1)
    lane_q = lax.broadcasted_iota(jnp.int32, (BLK, PAIR), 1)
    limit = jnp.where(
        row < BLK,
        lengths[block],
        jnp.where(row < 2 * BLK, lengths[partner] + BLK, known + 2 * BLK),
    )
    bias = jnp.where(row < limit, 0.0, -1e30).astype(jnp.float32)

    x_all = normed[...]
    dot = functools.partial(jnp.dot, preferred_element_type=jnp.float32)
    q = dot(normed[pl.ds(0, BLK), :], weights[step, 0])
    k = dot(x_all, weights[step, 1])
    v = dot(x_all, weights[step, 2]).astype(jnp.bfloat16)
    for pair in range(2):
        lanes = slice(pair * PAIR, (pair + 1) * PAIR)
        q_pair, k_pair, v_pair = q[:, lanes], k[:, lanes], v[:, lanes]
        parts = []
        for head in range(2):
            mine_q = (lane_q < HEAD_DIM) if head == 0 else (lane_q >= HEAD_DIM)
            free = HEAD_DIM if head == 0 else 0
            q_head = jnp.where(
                mine_q, q_pair, jnp.where(lane_q == free, 1.0, 0.0)
            ).astype(jnp.bfloat16)
            k_head = jnp.where(lane_k == free, bias, k_pair).astype(jnp.bfloat16)
            scores = lax.dot_general(
                q_head, k_head, (((1,), (1,)), ((), ())), preferred_element_type=jnp.float32
            )
            top = jnp.max(scores, axis=-1, keepdims=True)
            expo = jnp.exp2((scores - top) * SCALE_LOG2)
            total = jnp.sum(expo, axis=-1, keepdims=True)
            mixed = dot(expo.astype(jnp.bfloat16), v_pair)
            parts.append(mixed / total)
        both = jnp.where(lane_q < HEAD_DIM, parts[0], parts[1]).astype(jnp.bfloat16)
        half = core if pair == 0 else 1 - core
        place = pl.multiple_of((half * STEPS + step) * PAIR, PAIR)
        ctx[:, pl.ds(place, PAIR)] = both

    @pl.when(step == STEPS - 1)
    def _():
        if with_out:
            context = ctx[...]
            for half in range(2):
                target = out_weights.at[half]
                pltpu.make_async_copy(target, target, out_sems.at[half]).wait()
                update = dot(context, target[...])
                absolute = core if half == 0 else 1 - core
                if first_block:
                    place = pl.ds(pl.multiple_of(absolute * HALF, 128), HALF)
                    here_rows = own[:, place].astype(jnp.float32)
                    out[:, place] = (here_rows + update).astype(jnp.bfloat16)
                else:
                    place = pl.ds(pl.multiple_of(absolute * HALF, 128), HALF)
                    for part in range(2):
                        rows = pl.ds(part * HALO, HALO)
                        change = update[part * HALO : (part + 1) * HALO]
                        out[rows, place] = (slot_half(2 + part, absolute) + change).astype(
                            jnp.bfloat16
                        )
        else:
            out[...] = ctx[...]


def layer(scal, lengths, matchings, mine, yours, rows, first_block, with_out):
    hbm = pl.BlockSpec(memory_space=pl.ANY)
    whole = [pl.BlockSpec(r.shape, lambda i, *s: (0, 0)) for r in rows]
    scratch = [
        pltpu.VMEM((2 * BLK + HALO, D), jnp.bfloat16),
        pltpu.VMEM((BLK, D), jnp.bfloat16),
        pltpu.VMEM((STEPS, 3, D, 2 * PAIR), jnp.bfloat16),
        pltpu.SemaphoreType.DMA((STEPS, 3, 2)),
    ]
    if with_out:
        scratch += [
            pltpu.VMEM((2, D, HALF), jnp.bfloat16),
            pltpu.SemaphoreType.DMA((2,)),
            pltpu.VMEM((HALF // 128, 2048, 128), jnp.float32),
        ]
    return pl.pallas_call(
        functools.partial(layer_kernel, first_block, with_out),
        grid_spec=pltpu.PrefetchScalarGridSpec(
            num_scalar_prefetch=3,
            grid=(STEPS,),
            in_specs=[hbm] * (2 * PIECES) + whole,
            out_specs=pl.BlockSpec((BLK, D), lambda i, *s: (0, 0)),
            scratch_shapes=scratch,
        ),
        out_shape=jax.ShapeDtypeStruct((BLK, D), jnp.bfloat16),
        compiler_params=pltpu.CompilerParams(
            dimension_semantics=("arbitrary",), vmem_limit_bytes=60 * 1024 * 1024
        ),
        cost_estimate=pl.CostEstimate(
            flops=8 * 10**9, bytes_accessed=14 * 10**6, transcendentals=4 * 10**6
        ),
    )(scal, lengths, matchings, *mine, *yours, *rows)


def next_to(block):
    return lax.ppermute(block, ALL, X_UP), lax.ppermute(block, ALL, X_DOWN)


def across_x(block, below, above):
    far_top = lax.ppermute(below[: D // 2], ALL, X_UP)
    far_bottom = lax.ppermute(above[D // 2 :], ALL, X_DOWN)
    return block, above, far_top, far_bottom, below


def other_core(pieces):
    return tuple(lax.ppermute(piece, ALL, CORE_SWAP) for piece in pieces)


def gather_rows(wqkv, wout, x, core, y_hi):
    first = jnp.concatenate([wqkv[0], wout[0]], axis=1)
    second = wqkv[1].reshape(-1, 3, 2, HALF)

    def column_block(half):
        part_0 = lax.dynamic_slice_in_dim(first, (x * 2 + half) * HALF, HALF, 1)
        part_1 = lax.dynamic_index_in_dim(second, half, 2, keepdims=False).reshape(-1, 3 * HALF)
        part_1 = jnp.pad(part_1, ((0, 0), (0, 128)))
        return jnp.concatenate(
            [part_0, lax.dynamic_slice_in_dim(part_1, x * 512, 512, 1)], axis=1
        )

    keep, give = column_block(core), column_block(1 - core)
    near = lax.ppermute(give, ALL, CORE_SWAP)
    cross = lax.ppermute(keep, ALL, CROSS_SWAP)
    far = lax.ppermute(give, ALL, FAR_SWAP)

    def in_order(mine_first, mine, yours):
        return jnp.where(
            mine_first,
            jnp.concatenate([mine, yours], axis=0),
            jnp.concatenate([yours, mine], axis=0),
        )

    return in_order(
        y_hi == 0, in_order(core == 0, keep, near), in_order(core == 0, cross, far)
    )


def local(frames, lengths, matchings, wqkv, wout):
    gx, gy = lax.axis_index("gx"), lax.axis_index("gy")
    here = gx * 32 + gy
    core, y_hi, x = gy & 1, (gy >> 1) & 1, gx >> 1
    plane = gather_rows(wqkv, wout, x, core, y_hi)

    spread_in = frames.reshape(2, HALO, 2, HALF).transpose(2, 1, 0, 3).reshape(256, 2, HALF)
    plane, spread_in = lax.optimization_barrier((plane, spread_in))
    columns = lax.all_gather(plane, "gy", axis=0, tiled=True, axis_index_groups=Z_GROUPS)
    spread = lax.all_to_all(spread_in, ALL, 0, 0, tiled=True).reshape(512, HALF)

    partner_0, partner_1 = matchings[0], matchings[1]
    second = lookup_all(partner_0, partner_1)
    before = jnp.maximum(jnp.arange(256, dtype=jnp.int32) - 1, 0)
    before_1 = jnp.maximum(partner_1 - 1, 0)
    high = ((here & (HALO - 1)) < jnp.maximum(lengths - HALO, 0)).astype(jnp.int32)
    wanted = jnp.stack(
        [
            2 * partner_0,
            2 * partner_0 + 1,
            2 * partner_1,
            2 * partner_1 + 1,
            2 * second,
            2 * second + 1,
            2 * before_1 + lookup_all(high, before_1),
            2 * before + lookup_all(high, before),
        ],
        axis=1,
    ).reshape(-1)
    chosen = (wanted[:, None] == jnp.arange(512, dtype=jnp.int32)[None, :]).astype(jnp.bfloat16)
    spread, columns = lax.optimization_barrier((spread, columns))
    routed = jnp.dot(chosen, spread, preferred_element_type=jnp.float32).astype(jnp.bfloat16)
    collected = lax.all_to_all(routed.reshape(256, 8, HALF), ALL, 0, 0, tiled=True)
    collected = collected.reshape(2048, HALF)

    block_0, block_1 = columns[:, :HALF], columns[:, HALF:]
    mine_0 = across_x(block_0, *next_to(block_0))
    yours_0 = other_core(mine_0)
    block_1, mine_0 = lax.optimization_barrier((block_1, mine_0))
    near_1 = next_to(block_1)

    scal = jnp.stack([here, core, x]).astype(jnp.int32)
    run = functools.partial(layer, scal, lengths, matchings)
    hidden = run(mine_0, yours_0, (frames, collected), True, True)
    tail_start = jnp.maximum(lookup(lengths, here) - HALO, 0)
    own_tail = lax.dynamic_slice_in_dim(hidden, tail_start, HALO, 0)
    tail = lax.ppermute(own_tail, ALL, [(i, i + 1) for i in range(255)])
    near_1, hidden = lax.optimization_barrier((near_1, hidden))
    mine_1 = across_x(block_1, *near_1)
    hidden_1 = run(mine_0, yours_0, (collected,), False, True)
    far_1, hidden_1 = lax.optimization_barrier((mine_1[2:4], hidden_1))
    mine_1 = mine_1[:2] + far_1 + mine_1[4:]
    yours_1 = other_core(mine_1)
    context = run(mine_1, yours_1, (hidden, hidden_1, tail), True, False)
    return hidden, context


def solution(mesh):
    rows = P(ALL, None)
    return jax.shard_map(
        local,
        mesh=mesh,
        in_specs=(rows, P(), P(), P(None, "gy", None), P(None, "gy", None)),
        out_specs=(rows, rows),
        check_vma=False,
    )
```

```python
import functools
import math

import jax
import jax.numpy as jnp
from jax import lax
from jax.experimental import pallas as pl
from jax.experimental.pallas import tpu as pltpu
from jax.sharding import PartitionSpec as P

ALL = ("gx", "gy")
HEAD_DIM = 64
HALO = 128
BLK = 256
D = 1280
HALF = D // 2
PAIR = 2 * HEAD_DIM
STEPS = D // (2 * PAIR)
PIECES = 3
WIDTHS = (HALF, 512)
GATHERED = sum(WIDTHS)
SCALE_LOG2 = 0.125 * math.log2(math.e)


def flat_pairs(move):
    pairs = []
    for gx in range(8):
        for gy in range(32):
            x, y_lo, z, y_hi, core = move(gx // 2, gx % 2, gy // 4, (gy // 2) % 2, gy % 2)
            pairs.append((gx * 32 + gy, (x % 4 * 2 + y_lo) * 32 + z % 8 * 4 + y_hi * 2 + core))
    return pairs


CORE_SWAP = flat_pairs(lambda x, l, z, h, c: (x, l, z, h, 1 - c))
CROSS_SWAP = flat_pairs(lambda x, l, z, h, c: (x, 1 - l, z, 1 - h, c))
FAR_SWAP = flat_pairs(lambda x, l, z, h, c: (x, 1 - l, z, 1 - h, 1 - c))
X_UP = flat_pairs(lambda x, l, z, h, c: (x + 1, l, z, h, c))
X_DOWN = flat_pairs(lambda x, l, z, h, c: (x - 1, l, z, h, c))
Z_GROUPS = [[z * 4 + k for z in range(8)] for k in range(4)]


def lookup(table, index):
    return jnp.sum(jnp.where(jnp.arange(table.shape[0], dtype=jnp.int32) == index, table, 0))


def lookup_all(table, index):
    ids = jnp.arange(table.shape[0], dtype=jnp.int32)
    return jnp.sum(jnp.where(ids[None, :] == index[:, None], table[None, :], 0), axis=1)


def standardized(rows):
    values = rows.astype(jnp.float32)
    mean = jnp.mean(values, axis=-1, keepdims=True)
    centred = values - mean
    variance = jnp.mean(centred * centred, axis=-1, keepdims=True)
    return (centred * lax.rsqrt(variance + 1e-05)).astype(jnp.bfloat16)


def layer_kernel(first_block, with_out, scal, lengths, matchings, *refs):
    width_here = WIDTHS[0 if with_out else 1]
    tiles = width_here // PAIR
    own_at = 0 if with_out else WIDTHS[0]
    sources, refs = (refs[:PIECES], refs[PIECES : 2 * PIECES]), refs[2 * PIECES :]
    if first_block:
        own, refs = refs[0], refs[1:]
    if with_out:
        collected, out, normed, ctx, weights, weight_sems, out_weights, out_sems, spare = refs
    else:
        other, tail, out, normed, ctx, weights, weight_sems = refs
    step = pl.program_id(0)
    here, core, x = scal[0], scal[1], scal[2]
    block = here if first_block else matchings[1, here]
    partner = matchings[0 if with_out else 1, block]
    known = jnp.minimum(lengths[jnp.maximum(block - 1, 0)], HALO)
    known = jnp.where(block > 0, known, 0)

    def slot_half(at, half):
        rows = pl.ds(half * 1024 + at, HALO, stride=8)
        return jnp.concatenate([spare[i, rows, :] for i in range(HALF // 128)], axis=1)

    def start_tile(half, x_here, index, target, width, sem):
        place = (index // tiles - x_here) % 4
        column = index % tiles * PAIR
        if place % 2 == 0:
            piece = 0
            column += own_at + place // 2 * GATHERED
        else:
            piece = 1 + place // 2
        source = sources[half][piece].at[:, pl.ds(column, width)]
        pltpu.make_async_copy(source, target, sem).start()

    @pl.when(step == 0)
    def _():
        for x_here in range(4):

            @pl.when(x == x_here)
            def _():
                for at in range(STEPS):
                    for kind in range(3):
                        for half in range(2):
                            start_tile(
                                half,
                                x_here,
                                kind * STEPS + at,
                                weights.at[at, kind, :, pl.ds(half * PAIR, PAIR)],
                                PAIR,
                                weight_sems.at[at, kind, half],
                            )
                if with_out:
                    for half in range(2):
                        start_tile(
                            half, x_here, 3 * STEPS, out_weights.at[half], HALF, out_sems.at[half]
                        )

        if with_out:
            for lane_tile in range(HALF // 128):
                lanes = pl.ds(lane_tile * 128, 128)
                spare[lane_tile] = collected[:, lanes].astype(jnp.float32)

            def slot(at):
                return jnp.concatenate([slot_half(at, 0), slot_half(at, 1)], axis=1)

            slots = (0, 1, 7) if first_block else (2, 3, 4, 5, 6)
            if first_block:
                normed[pl.ds(0, BLK), :] = standardized(own[...])
            base = BLK if first_block else 0
            for order, at in enumerate(slots):
                normed[pl.ds(base + order * HALO, HALO), :] = standardized(slot(at))
        else:
            normed[pl.ds(0, BLK), :] = standardized(own[...])
            normed[pl.ds(BLK, BLK), :] = standardized(other[...])
            normed[pl.ds(2 * BLK, HALO), :] = standardized(tail[...])

    for kind in range(3):
        for half in range(2):
            target = weights.at[step, kind, :, pl.ds(half * PAIR, PAIR)]
            pltpu.make_async_copy(target, target, weight_sems.at[step, kind, half]).wait()

    count = 2 * BLK + HALO
    row = lax.broadcasted_iota(jnp.int32, (count, PAIR), 0)
    lane_k = lax.broadcasted_iota(jnp.int32, (count, PAIR), 1)
    lane_q = lax.broadcasted_iota(jnp.int32, (BLK, PAIR), 1)
    limit = jnp.where(
        row < BLK,
        lengths[block],
        jnp.where(row < 2 * BLK, lengths[partner] + BLK, known + 2 * BLK),
    )
    bias = jnp.where(row < limit, 0.0, -1e30).astype(jnp.float32)

    x_all = normed[...]
    dot = functools.partial(jnp.dot, preferred_element_type=jnp.float32)
    q = dot(normed[pl.ds(0, BLK), :], weights[step, 0])
    k = dot(x_all, weights[step, 1])
    v = dot(x_all, weights[step, 2]).astype(jnp.bfloat16)
    for pair in range(2):
        lanes = slice(pair * PAIR, (pair + 1) * PAIR)
        q_pair, k_pair, v_pair = q[:, lanes], k[:, lanes], v[:, lanes]
        parts = []
        for head in range(2):
            mine_q = (lane_q < HEAD_DIM) if head == 0 else (lane_q >= HEAD_DIM)
            free = HEAD_DIM if head == 0 else 0
            q_head = jnp.where(
                mine_q, q_pair, jnp.where(lane_q == free, 1.0, 0.0)
            ).astype(jnp.bfloat16)
            k_head = jnp.where(lane_k == free, bias, k_pair).astype(jnp.bfloat16)
            scores = lax.dot_general(
                q_head, k_head, (((1,), (1,)), ((), ())), preferred_element_type=jnp.float32
            )
            top = jnp.max(scores, axis=-1, keepdims=True)
            expo = jnp.exp2((scores - top) * SCALE_LOG2)
            total = jnp.sum(expo, axis=-1, keepdims=True)
            mixed = dot(expo.astype(jnp.bfloat16), v_pair)
            parts.append(mixed / total)
        both = jnp.where(lane_q < HEAD_DIM, parts[0], parts[1]).astype(jnp.bfloat16)
        half = core if pair == 0 else 1 - core
        place = pl.multiple_of((half * STEPS + step) * PAIR, PAIR)
        ctx[:, pl.ds(place, PAIR)] = both

    @pl.when(step == STEPS - 1)
    def _():
        if with_out:
            context = ctx[...]
            for half in range(2):
                target = out_weights.at[half]
                pltpu.make_async_copy(target, target, out_sems.at[half]).wait()
                update = dot(context, target[...])
                absolute = core if half == 0 else 1 - core
                if first_block:
                    place = pl.ds(pl.multiple_of(absolute * HALF, 128), HALF)
                    here_rows = own[:, place].astype(jnp.float32)
                    out[:, place] = (here_rows + update).astype(jnp.bfloat16)
                else:
                    place = pl.ds(pl.multiple_of(absolute * HALF, 128), HALF)
                    for part in range(2):
                        rows = pl.ds(part * HALO, HALO)
                        change = update[part * HALO : (part + 1) * HALO]
                        out[rows, place] = (slot_half(2 + part, absolute) + change).astype(
                            jnp.bfloat16
                        )
        else:
            out[...] = ctx[...]


def layer(scal, lengths, matchings, mine, yours, rows, first_block, with_out):
    hbm = pl.BlockSpec(memory_space=pl.ANY)
    whole = [pl.BlockSpec(r.shape, lambda i, *s: (0, 0)) for r in rows]
    scratch = [
        pltpu.VMEM((2 * BLK + HALO, D), jnp.bfloat16),
        pltpu.VMEM((BLK, D), jnp.bfloat16),
        pltpu.VMEM((STEPS, 3, D, 2 * PAIR), jnp.bfloat16),
        pltpu.SemaphoreType.DMA((STEPS, 3, 2)),
    ]
    if with_out:
        scratch += [
            pltpu.VMEM((2, D, HALF), jnp.bfloat16),
            pltpu.SemaphoreType.DMA((2,)),
            pltpu.VMEM((HALF // 128, 2048, 128), jnp.float32),
        ]
    return pl.pallas_call(
        functools.partial(layer_kernel, first_block, with_out),
        grid_spec=pltpu.PrefetchScalarGridSpec(
            num_scalar_prefetch=3,
            grid=(STEPS,),
            in_specs=[hbm] * (2 * PIECES) + whole,
            out_specs=pl.BlockSpec((BLK, D), lambda i, *s: (0, 0)),
            scratch_shapes=scratch,
        ),
        out_shape=jax.ShapeDtypeStruct((BLK, D), jnp.bfloat16),
        compiler_params=pltpu.CompilerParams(
            dimension_semantics=("arbitrary",), vmem_limit_bytes=60 * 1024 * 1024
        ),
        cost_estimate=pl.CostEstimate(
            flops=8 * 10**9, bytes_accessed=14 * 10**6, transcendentals=4 * 10**6
        ),
    )(scal, lengths, matchings, *mine, *yours, *rows)


def next_to(block):
    return lax.ppermute(block, ALL, X_DOWN), lax.ppermute(block, ALL, X_UP)


def other_core(pieces):
    return tuple(lax.ppermute(piece, ALL, CORE_SWAP) for piece in pieces)


def gather_rows(wqkv, wout, x, core, y_hi):
    first = jnp.concatenate([wqkv[0], wout[0]], axis=1)
    second = wqkv[1].reshape(-1, 3, 2, HALF)

    def column_block(half):
        part_1 = lax.dynamic_index_in_dim(second, half, 2, keepdims=False).reshape(-1, 3 * HALF)
        part_1 = jnp.pad(part_1, ((0, 0), (0, 128)))
        parts = []
        for place in (x, (x + 2) & 3):
            parts.append(lax.dynamic_slice_in_dim(first, (place * 2 + half) * HALF, HALF, 1))
            parts.append(lax.dynamic_slice_in_dim(part_1, place * WIDTHS[1], WIDTHS[1], 1))
        return jnp.concatenate(parts, axis=1)

    keep, give = column_block(core), column_block(1 - core)
    near = lax.ppermute(give, ALL, CORE_SWAP)
    cross = lax.ppermute(keep, ALL, CROSS_SWAP)
    far = lax.ppermute(give, ALL, FAR_SWAP)

    def in_order(mine_first, mine, yours):
        return jnp.where(
            mine_first,
            jnp.concatenate([mine, yours], axis=0),
            jnp.concatenate([yours, mine], axis=0),
        )

    return in_order(
        y_hi == 0, in_order(core == 0, keep, near), in_order(core == 0, cross, far)
    )


def local(frames, lengths, matchings, wqkv, wout):
    gx, gy = lax.axis_index("gx"), lax.axis_index("gy")
    here = gx * 32 + gy
    core, y_hi, x = gy & 1, (gy >> 1) & 1, gx >> 1
    plane = gather_rows(wqkv, wout, x, core, y_hi)

    spread_in = frames.reshape(2, HALO, 2, HALF).transpose(2, 1, 0, 3).reshape(256, 2, HALF)
    plane, spread_in = lax.optimization_barrier((plane, spread_in))
    columns = lax.all_gather(plane, "gy", axis=0, tiled=True, axis_index_groups=Z_GROUPS)
    spread = lax.all_to_all(spread_in, ALL, 0, 0, tiled=True).reshape(512, HALF)

    partner_0, partner_1 = matchings[0], matchings[1]
    second = lookup_all(partner_0, partner_1)
    before = jnp.maximum(jnp.arange(256, dtype=jnp.int32) - 1, 0)
    before_1 = jnp.maximum(partner_1 - 1, 0)
    high = ((here & (HALO - 1)) < jnp.maximum(lengths - HALO, 0)).astype(jnp.int32)
    wanted = jnp.stack(
        [
            2 * partner_0,
            2 * partner_0 + 1,
            2 * partner_1,
            2 * partner_1 + 1,
            2 * second,
            2 * second + 1,
            2 * before_1 + lookup_all(high, before_1),
            2 * before + lookup_all(high, before),
        ],
        axis=1,
    ).reshape(-1)
    chosen = (wanted[:, None] == jnp.arange(512, dtype=jnp.int32)[None, :]).astype(jnp.bfloat16)
    routed = jnp.dot(chosen, spread, preferred_element_type=jnp.float32).astype(jnp.bfloat16)
    columns, _ = lax.optimization_barrier((columns, routed))
    collected = lax.all_to_all(routed.reshape(256, 8, HALF), ALL, 0, 0, tiled=True)
    collected = collected.reshape(2048, HALF)

    yours = lax.ppermute(columns, ALL, CORE_SWAP)
    near_0 = next_to(columns[:, : WIDTHS[0]])
    mine_0, yours_0 = (columns, *near_0), (yours, *other_core(near_0))
    block_1, near_0 = lax.optimization_barrier((columns[:, WIDTHS[0] : GATHERED], near_0))
    near_1 = next_to(block_1)

    scal = jnp.stack([here, core, x]).astype(jnp.int32)
    run = functools.partial(layer, scal, lengths, matchings)
    hidden = run(mine_0, yours_0, (frames, collected), True, True)
    tail_start = jnp.maximum(lookup(lengths, here) - HALO, 0)
    own_tail = lax.dynamic_slice_in_dim(hidden, tail_start, HALO, 0)
    tail = lax.ppermute(own_tail, ALL, [(i, i + 1) for i in range(255)])
    near_1, hidden = lax.optimization_barrier((near_1, hidden))
    mine_1, yours_1 = (columns, *near_1), (yours, *other_core(near_1))
    hidden_1 = run(mine_0, yours_0, (collected,), False, True)
    context = run(mine_1, yours_1, (hidden, hidden_1, tail), True, False)
    return hidden, context


def solution(mesh):
    rows = P(ALL, None)
    return jax.shard_map(
        local,
        mesh=mesh,
        in_specs=(rows, P(), P(), P(None, "gy", None), P(None, "gy", None)),
        out_specs=(rows, rows),
        check_vma=False,
    )
```

```python
import functools
import math

import jax
import jax.numpy as jnp
from jax import lax
from jax.experimental import pallas as pl
from jax.experimental.pallas import tpu as pltpu
from jax.sharding import PartitionSpec as P

ALL = ("gx", "gy")
HEAD_DIM = 64
HALO = 128
BLK = 256
D = 1280
HALF = D // 2
PAIR = 2 * HEAD_DIM
STEPS = D // (2 * PAIR)
PIECES = 3
WIDTHS = (HALF, 512)
SCALE_LOG2 = 0.125 * math.log2(math.e)


def flat_pairs(move):
    pairs = []
    for gx in range(8):
        for gy in range(32):
            x, y_lo, z, y_hi, core = move(gx // 2, gx % 2, gy // 4, (gy // 2) % 2, gy % 2)
            pairs.append((gx * 32 + gy, (x % 4 * 2 + y_lo) * 32 + z % 8 * 4 + y_hi * 2 + core))
    return pairs


CORE_SWAP = flat_pairs(lambda x, l, z, h, c: (x, l, z, h, 1 - c))
CROSS_SWAP = flat_pairs(lambda x, l, z, h, c: (x, 1 - l, z, 1 - h, c))
FAR_SWAP = flat_pairs(lambda x, l, z, h, c: (x, 1 - l, z, 1 - h, 1 - c))
X_UP = flat_pairs(lambda x, l, z, h, c: (x + 1, l, z, h, c))
X_DOWN = flat_pairs(lambda x, l, z, h, c: (x - 1, l, z, h, c))
Z_GROUPS = [[z * 4 + k for z in range(8)] for k in range(4)]


def lookup(table, index):
    return jnp.sum(jnp.where(jnp.arange(table.shape[0], dtype=jnp.int32) == index, table, 0))


def lookup_all(table, index):
    ids = jnp.arange(table.shape[0], dtype=jnp.int32)
    return jnp.sum(jnp.where(ids[None, :] == index[:, None], table[None, :], 0), axis=1)


def standardized(rows):
    values = rows.astype(jnp.float32)
    mean = jnp.mean(values, axis=-1, keepdims=True)
    centred = values - mean
    variance = jnp.mean(centred * centred, axis=-1, keepdims=True)
    return (centred * lax.rsqrt(variance + 1e-05)).astype(jnp.bfloat16)


def layer_kernel(first_block, with_out, scal, lengths, matchings, *refs):
    width_here = WIDTHS[0 if with_out else 1]
    tiles = width_here // PAIR
    sources, refs = (refs[:PIECES], refs[PIECES : 2 * PIECES]), refs[2 * PIECES :]
    if first_block:
        own, refs = refs[0], refs[1:]
    if with_out:
        collected, out, normed, ctx, weights, weight_sems, out_weights, out_sems, spare = refs
    else:
        other, tail, out, normed, ctx, weights, weight_sems = refs
    step = pl.program_id(0)
    here, core, x = scal[0], scal[1], scal[2]
    block = here if first_block else matchings[1, here]
    partner = matchings[0 if with_out else 1, block]
    known = jnp.minimum(lengths[jnp.maximum(block - 1, 0)], HALO)
    known = jnp.where(block > 0, known, 0)

    def slot_half(at, half):
        rows = pl.ds(half * 1024 + at, HALO, stride=8)
        return jnp.concatenate([spare[i, rows, :] for i in range(HALF // 128)], axis=1)

    def start_tile(half, x_here, index, target, width, sem):
        place = (index // tiles - x_here) % 4
        column = index % tiles * PAIR
        if place % 2 == 0:
            piece = 0
            column += place // 2 * width_here
        else:
            piece = 1 + place // 2
        source = sources[half][piece].at[:, pl.ds(column, width)]
        pltpu.make_async_copy(source, target, sem).start()

    @pl.when(step == 0)
    def _():
        for x_here in range(4):

            @pl.when(x == x_here)
            def _():
                for at in range(STEPS):
                    for kind in range(3):
                        for half in range(2):
                            start_tile(
                                half,
                                x_here,
                                kind * STEPS + at,
                                weights.at[at, kind, :, pl.ds(half * PAIR, PAIR)],
                                PAIR,
                                weight_sems.at[at, kind, half],
                            )
                if with_out:
                    for half in range(2):
                        start_tile(
                            half, x_here, 3 * STEPS, out_weights.at[half], HALF, out_sems.at[half]
                        )

        if with_out:
            for lane_tile in range(HALF // 128):
                lanes = pl.ds(lane_tile * 128, 128)
                spare[lane_tile] = collected[:, lanes].astype(jnp.float32)

            def slot(at):
                return jnp.concatenate([slot_half(at, 0), slot_half(at, 1)], axis=1)

            slots = (0, 1, 7) if first_block else (2, 3, 4, 5, 6)
            if first_block:
                normed[pl.ds(0, BLK), :] = standardized(own[...])
            base = BLK if first_block else 0
            for order, at in enumerate(slots):
                normed[pl.ds(base + order * HALO, HALO), :] = standardized(slot(at))
        else:
            normed[pl.ds(0, BLK), :] = standardized(own[...])
            normed[pl.ds(BLK, BLK), :] = standardized(other[...])
            normed[pl.ds(2 * BLK, HALO), :] = standardized(tail[...])

    for kind in range(3):
        for half in range(2):
            target = weights.at[step, kind, :, pl.ds(half * PAIR, PAIR)]
            pltpu.make_async_copy(target, target, weight_sems.at[step, kind, half]).wait()

    count = 2 * BLK + HALO
    row = lax.broadcasted_iota(jnp.int32, (count, PAIR), 0)
    lane_k = lax.broadcasted_iota(jnp.int32, (count, PAIR), 1)
    lane_q = lax.broadcasted_iota(jnp.int32, (BLK, PAIR), 1)
    limit = jnp.where(
        row < BLK,
        lengths[block],
        jnp.where(row < 2 * BLK, lengths[partner] + BLK, known + 2 * BLK),
    )
    bias = jnp.where(row < limit, 0.0, -1e30).astype(jnp.float32)

    x_all = normed[...]
    dot = functools.partial(jnp.dot, preferred_element_type=jnp.float32)
    q = dot(normed[pl.ds(0, BLK), :], weights[step, 0])
    k = dot(x_all, weights[step, 1])
    v = dot(x_all, weights[step, 2]).astype(jnp.bfloat16)
    for pair in range(2):
        lanes = slice(pair * PAIR, (pair + 1) * PAIR)
        q_pair, k_pair, v_pair = q[:, lanes], k[:, lanes], v[:, lanes]
        parts = []
        for head in range(2):
            mine_q = (lane_q < HEAD_DIM) if head == 0 else (lane_q >= HEAD_DIM)
            free = HEAD_DIM if head == 0 else 0
            q_head = jnp.where(
                mine_q, q_pair, jnp.where(lane_q == free, 1.0, 0.0)
            ).astype(jnp.bfloat16)
            k_head = jnp.where(lane_k == free, bias, k_pair).astype(jnp.bfloat16)
            scores = lax.dot_general(
                q_head, k_head, (((1,), (1,)), ((), ())), preferred_element_type=jnp.float32
            )
            top = jnp.max(scores, axis=-1, keepdims=True)
            expo = jnp.exp2((scores - top) * SCALE_LOG2)
            total = jnp.sum(expo, axis=-1, keepdims=True)
            mixed = dot(expo.astype(jnp.bfloat16), v_pair)
            parts.append(mixed / total)
        both = jnp.where(lane_q < HEAD_DIM, parts[0], parts[1]).astype(jnp.bfloat16)
        half = core if pair == 0 else 1 - core
        place = pl.multiple_of((half * STEPS + step) * PAIR, PAIR)
        ctx[:, pl.ds(place, PAIR)] = both

    @pl.when(step == STEPS - 1)
    def _():
        if with_out:
            context = ctx[...]
            for half in range(2):
                target = out_weights.at[half]
                pltpu.make_async_copy(target, target, out_sems.at[half]).wait()
                update = dot(context, target[...])
                absolute = core if half == 0 else 1 - core
                if first_block:
                    place = pl.ds(pl.multiple_of(absolute * HALF, 128), HALF)
                    here_rows = own[:, place].astype(jnp.float32)
                    out[:, place] = (here_rows + update).astype(jnp.bfloat16)
                else:
                    place = pl.ds(pl.multiple_of(absolute * HALF, 128), HALF)
                    for part in range(2):
                        rows = pl.ds(part * HALO, HALO)
                        change = update[part * HALO : (part + 1) * HALO]
                        out[rows, place] = (slot_half(2 + part, absolute) + change).astype(
                            jnp.bfloat16
                        )
        else:
            out[...] = ctx[...]


def layer(scal, lengths, matchings, mine, yours, rows, first_block, with_out):
    hbm = pl.BlockSpec(memory_space=pl.ANY)
    whole = [pl.BlockSpec(r.shape, lambda i, *s: (0, 0)) for r in rows]
    scratch = [
        pltpu.VMEM((2 * BLK + HALO, D), jnp.bfloat16),
        pltpu.VMEM((BLK, D), jnp.bfloat16),
        pltpu.VMEM((STEPS, 3, D, 2 * PAIR), jnp.bfloat16),
        pltpu.SemaphoreType.DMA((STEPS, 3, 2)),
    ]
    if with_out:
        scratch += [
            pltpu.VMEM((2, D, HALF), jnp.bfloat16),
            pltpu.SemaphoreType.DMA((2,)),
            pltpu.VMEM((HALF // 128, 2048, 128), jnp.float32),
        ]
    return pl.pallas_call(
        functools.partial(layer_kernel, first_block, with_out),
        grid_spec=pltpu.PrefetchScalarGridSpec(
            num_scalar_prefetch=3,
            grid=(STEPS,),
            in_specs=[hbm] * (2 * PIECES) + whole,
            out_specs=pl.BlockSpec((BLK, D), lambda i, *s: (0, 0)),
            scratch_shapes=scratch,
        ),
        out_shape=jax.ShapeDtypeStruct((BLK, D), jnp.bfloat16),
        compiler_params=pltpu.CompilerParams(
            dimension_semantics=("arbitrary",), vmem_limit_bytes=60 * 1024 * 1024
        ),
        cost_estimate=pl.CostEstimate(
            flops=8 * 10**9, bytes_accessed=14 * 10**6, transcendentals=4 * 10**6
        ),
    )(scal, lengths, matchings, *mine, *yours, *rows)


def next_to(block):
    return lax.ppermute(block, ALL, X_DOWN), lax.ppermute(block, ALL, X_UP)


def other_core(pieces):
    return tuple(lax.ppermute(piece, ALL, CORE_SWAP) for piece in pieces)


def gather_rows(wqkv, wout, x, core, y_hi):
    first = jnp.concatenate([wqkv[0], wout[0]], axis=1)
    second = wqkv[1].reshape(-1, 3, 2, HALF)

    def column_block(half):
        part_1 = lax.dynamic_index_in_dim(second, half, 2, keepdims=False).reshape(-1, 3 * HALF)
        part_1 = jnp.pad(part_1, ((0, 0), (0, 128)))
        places = (x, (x + 2) & 3)
        starts = [(first, (place * 2 + half) * HALF, HALF) for place in places]
        starts += [(part_1, place * WIDTHS[1], WIDTHS[1]) for place in places]
        return jnp.concatenate([lax.dynamic_slice_in_dim(a, i, n, 1) for a, i, n in starts], axis=1)

    keep, give = column_block(core), column_block(1 - core)
    near = lax.ppermute(give, ALL, CORE_SWAP)
    cross = lax.ppermute(keep, ALL, CROSS_SWAP)
    far = lax.ppermute(give, ALL, FAR_SWAP)

    def in_order(mine_first, mine, yours):
        return jnp.where(
            mine_first,
            jnp.concatenate([mine, yours], axis=0),
            jnp.concatenate([yours, mine], axis=0),
        )

    return in_order(
        y_hi == 0, in_order(core == 0, keep, near), in_order(core == 0, cross, far)
    )


def local(frames, lengths, matchings, wqkv, wout):
    gx, gy = lax.axis_index("gx"), lax.axis_index("gy")
    here = gx * 32 + gy
    core, y_hi, x = gy & 1, (gy >> 1) & 1, gx >> 1
    plane = gather_rows(wqkv, wout, x, core, y_hi)

    spread_in = frames.reshape(2, HALO, 2, HALF).transpose(2, 1, 0, 3).reshape(256, 2, HALF)
    plane, spread_in = lax.optimization_barrier((plane, spread_in))
    columns_0, columns_1 = (
        lax.all_gather(part, "gy", axis=0, tiled=True, axis_index_groups=Z_GROUPS)
        for part in (plane[:, : 2 * WIDTHS[0]], plane[:, 2 * WIDTHS[0] :])
    )
    spread = lax.all_to_all(spread_in, ALL, 0, 0, tiled=True).reshape(512, HALF)

    partner_0, partner_1 = matchings[0], matchings[1]
    second = lookup_all(partner_0, partner_1)
    before = jnp.maximum(jnp.arange(256, dtype=jnp.int32) - 1, 0)
    before_1 = jnp.maximum(partner_1 - 1, 0)
    high = ((here & (HALO - 1)) < jnp.maximum(lengths - HALO, 0)).astype(jnp.int32)
    wanted = jnp.stack(
        [
            2 * partner_0,
            2 * partner_0 + 1,
            2 * partner_1,
            2 * partner_1 + 1,
            2 * second,
            2 * second + 1,
            2 * before_1 + lookup_all(high, before_1),
            2 * before + lookup_all(high, before),
        ],
        axis=1,
    ).reshape(-1)
    chosen = (wanted[:, None] == jnp.arange(512, dtype=jnp.int32)[None, :]).astype(jnp.bfloat16)
    routed = jnp.dot(chosen, spread, preferred_element_type=jnp.float32).astype(jnp.bfloat16)
    columns_0, _ = lax.optimization_barrier((columns_0, routed))
    collected = lax.all_to_all(routed.reshape(256, 8, HALF), ALL, 0, 0, tiled=True)
    collected = collected.reshape(2048, HALF)

    near_0 = next_to(columns_0[:, : WIDTHS[0]])
    mine_0 = (columns_0, *near_0)
    yours_0 = other_core(mine_0)
    columns_1, near_0 = lax.optimization_barrier((columns_1, near_0))
    near_1 = next_to(columns_1[:, : WIDTHS[1]])

    scal = jnp.stack([here, core, x]).astype(jnp.int32)
    run = functools.partial(layer, scal, lengths, matchings)
    hidden = run(mine_0, yours_0, (frames, collected), True, True)
    tail_start = jnp.maximum(lookup(lengths, here) - HALO, 0)
    own_tail = lax.dynamic_slice_in_dim(hidden, tail_start, HALO, 0)
    tail = lax.ppermute(own_tail, ALL, [(i, i + 1) for i in range(255)])
    near_1, hidden = lax.optimization_barrier((near_1, hidden))
    mine_1 = (columns_1, *near_1)
    yours_1 = other_core(mine_1)
    hidden_1 = run(mine_0, yours_0, (collected,), False, True)
    context = run(mine_1, yours_1, (hidden, hidden_1, tail), True, False)
    return hidden, context


def solution(mesh):
    rows = P(ALL, None)
    return jax.shard_map(
        local,
        mesh=mesh,
        in_specs=(rows, P(), P(), P(None, "gy", None), P(None, "gy", None)),
        out_specs=(rows, rows),
        check_vma=False,
    )
```

```python
import functools
import math

import jax
import jax.numpy as jnp
from jax import lax
from jax.experimental import pallas as pl
from jax.experimental.pallas import tpu as pltpu
from jax.sharding import PartitionSpec as P

ALL = ("gx", "gy")
HEAD_DIM = 64
HALO = 128
BLK = 256
D = 1280
HALF = D // 2
PAIR = 2 * HEAD_DIM
STEPS = D // (2 * PAIR)
PIECES = 3
WIDTHS = (HALF, 512)
SCALE_LOG2 = 0.125 * math.log2(math.e)


def flat_pairs(move):
    pairs = []
    for gx in range(8):
        for gy in range(32):
            x, y_lo, z, y_hi, core = move(gx // 2, gx % 2, gy // 4, (gy // 2) % 2, gy % 2)
            pairs.append((gx * 32 + gy, (x % 4 * 2 + y_lo) * 32 + z % 8 * 4 + y_hi * 2 + core))
    return pairs


CORE_SWAP = flat_pairs(lambda x, l, z, h, c: (x, l, z, h, 1 - c))
CROSS_SWAP = flat_pairs(lambda x, l, z, h, c: (x, 1 - l, z, 1 - h, c))
FAR_SWAP = flat_pairs(lambda x, l, z, h, c: (x, 1 - l, z, 1 - h, 1 - c))
X_UP = flat_pairs(lambda x, l, z, h, c: (x + 1, l, z, h, c))
X_DOWN = flat_pairs(lambda x, l, z, h, c: (x - 1, l, z, h, c))
Z_GROUPS = [[z * 4 + k for z in range(8)] for k in range(4)]


def lookup(table, index):
    return jnp.sum(jnp.where(jnp.arange(table.shape[0], dtype=jnp.int32) == index, table, 0))


def lookup_all(table, index):
    ids = jnp.arange(table.shape[0], dtype=jnp.int32)
    return jnp.sum(jnp.where(ids[None, :] == index[:, None], table[None, :], 0), axis=1)


def standardized(rows):
    values = rows.astype(jnp.float32)
    mean = jnp.mean(values, axis=-1, keepdims=True)
    centred = values - mean
    variance = jnp.mean(centred * centred, axis=-1, keepdims=True)
    return (centred * lax.rsqrt(variance + 1e-05)).astype(jnp.bfloat16)


def layer_kernel(first_block, with_out, scal, lengths, matchings, *refs):
    width_here = WIDTHS[0 if with_out else 1]
    tiles = width_here // PAIR
    sources, refs = (refs[:PIECES], refs[PIECES : 2 * PIECES]), refs[2 * PIECES :]
    if first_block:
        own, refs = refs[0], refs[1:]
    if with_out:
        collected, out, normed, ctx, weights, weight_sems, out_weights, out_sems, spare = refs
    else:
        other, tail, out, normed, ctx, weights, weight_sems = refs
    step = pl.program_id(0)
    here, core, x = scal[0], scal[1], scal[2]
    block = here if first_block else matchings[1, here]
    partner = matchings[0 if with_out else 1, block]
    known = jnp.minimum(lengths[jnp.maximum(block - 1, 0)], HALO)
    known = jnp.where(block > 0, known, 0)

    def slot_half(at, half):
        rows = pl.ds(half * 1024 + at, HALO, stride=8)
        return jnp.concatenate([spare[i, rows, :] for i in range(HALF // 128)], axis=1)

    def start_tile(half, x_here, index, target, width, sem):
        place = (index // tiles - x_here) % 4
        column = index % tiles * PAIR
        if place % 2 == 0:
            piece = 0
            column += place // 2 * width_here
        else:
            piece = 1 + place // 2
        source = sources[half][piece].at[:, pl.ds(column, width)]
        pltpu.make_async_copy(source, target, sem).start()

    @pl.when(step == 0)
    def _():
        for x_here in range(4):

            @pl.when(x == x_here)
            def _():
                for at in range(STEPS):
                    for kind in range(3):
                        for half in range(2):
                            start_tile(
                                half,
                                x_here,
                                kind * STEPS + at,
                                weights.at[at, kind, :, pl.ds(half * PAIR, PAIR)],
                                PAIR,
                                weight_sems.at[at, kind, half],
                            )
                if with_out:
                    for half in range(2):
                        start_tile(
                            half, x_here, 3 * STEPS, out_weights.at[half], HALF, out_sems.at[half]
                        )

        if with_out:
            for lane_tile in range(HALF // 128):
                lanes = pl.ds(lane_tile * 128, 128)
                spare[lane_tile] = collected[:, lanes].astype(jnp.float32)

            def slot(at):
                return jnp.concatenate([slot_half(at, 0), slot_half(at, 1)], axis=1)

            slots = (0, 1, 7) if first_block else (2, 3, 4, 5, 6)
            if first_block:
                normed[pl.ds(0, BLK), :] = standardized(own[...])
            base = BLK if first_block else 0
            for order, at in enumerate(slots):
                normed[pl.ds(base + order * HALO, HALO), :] = standardized(slot(at))
        else:
            normed[pl.ds(0, BLK), :] = standardized(own[...])
            normed[pl.ds(BLK, BLK), :] = standardized(other[...])
            normed[pl.ds(2 * BLK, HALO), :] = standardized(tail[...])

    for kind in range(3):
        for half in range(2):
            target = weights.at[step, kind, :, pl.ds(half * PAIR, PAIR)]
            pltpu.make_async_copy(target, target, weight_sems.at[step, kind, half]).wait()

    count = 2 * BLK + HALO
    row = lax.broadcasted_iota(jnp.int32, (count, PAIR), 0)
    lane_k = lax.broadcasted_iota(jnp.int32, (count, PAIR), 1)
    lane_q = lax.broadcasted_iota(jnp.int32, (BLK, PAIR), 1)
    limit = jnp.where(
        row < BLK,
        lengths[block],
        jnp.where(row < 2 * BLK, lengths[partner] + BLK, known + 2 * BLK),
    )
    bias = jnp.where(row < limit, 0.0, -1e30).astype(jnp.float32)

    x_all = normed[...]
    dot = functools.partial(jnp.dot, preferred_element_type=jnp.float32)
    q = dot(normed[pl.ds(0, BLK), :], weights[step, 0])
    k = dot(x_all, weights[step, 1])
    v = dot(x_all, weights[step, 2]).astype(jnp.bfloat16)
    for pair in range(2):
        lanes = slice(pair * PAIR, (pair + 1) * PAIR)
        q_pair, k_pair, v_pair = q[:, lanes], k[:, lanes], v[:, lanes]
        parts = []
        for head in range(2):
            mine_q = (lane_q < HEAD_DIM) if head == 0 else (lane_q >= HEAD_DIM)
            free = HEAD_DIM if head == 0 else 0
            q_head = jnp.where(
                mine_q, q_pair, jnp.where(lane_q == free, 1.0, 0.0)
            ).astype(jnp.bfloat16)
            k_head = jnp.where(lane_k == free, bias, k_pair).astype(jnp.bfloat16)
            scores = lax.dot_general(
                q_head, k_head, (((1,), (1,)), ((), ())), preferred_element_type=jnp.float32
            )
            top = jnp.max(scores, axis=-1, keepdims=True)
            expo = jnp.exp2((scores - top) * SCALE_LOG2)
            total = jnp.sum(expo, axis=-1, keepdims=True)
            mixed = dot(expo.astype(jnp.bfloat16), v_pair)
            parts.append(mixed / total)
        both = jnp.where(lane_q < HEAD_DIM, parts[0], parts[1]).astype(jnp.bfloat16)
        half = core if pair == 0 else 1 - core
        place = pl.multiple_of((half * STEPS + step) * PAIR, PAIR)
        ctx[:, pl.ds(place, PAIR)] = both

    @pl.when(step == STEPS - 1)
    def _():
        if with_out:
            context = ctx[...]
            for half in range(2):
                target = out_weights.at[half]
                pltpu.make_async_copy(target, target, out_sems.at[half]).wait()
                update = dot(context, target[...])
                absolute = core if half == 0 else 1 - core
                if first_block:
                    place = pl.ds(pl.multiple_of(absolute * HALF, 128), HALF)
                    here_rows = own[:, place].astype(jnp.float32)
                    out[:, place] = (here_rows + update).astype(jnp.bfloat16)
                else:
                    place = pl.ds(pl.multiple_of(absolute * HALF, 128), HALF)
                    for part in range(2):
                        rows = pl.ds(part * HALO, HALO)
                        change = update[part * HALO : (part + 1) * HALO]
                        out[rows, place] = (slot_half(2 + part, absolute) + change).astype(
                            jnp.bfloat16
                        )
        else:
            out[...] = ctx[...]


def layer(scal, lengths, matchings, mine, yours, rows, first_block, with_out):
    hbm = pl.BlockSpec(memory_space=pl.ANY)
    whole = [pl.BlockSpec(r.shape, lambda i, *s: (0, 0)) for r in rows]
    scratch = [
        pltpu.VMEM((2 * BLK + HALO, D), jnp.bfloat16),
        pltpu.VMEM((BLK, D), jnp.bfloat16),
        pltpu.VMEM((STEPS, 3, D, 2 * PAIR), jnp.bfloat16),
        pltpu.SemaphoreType.DMA((STEPS, 3, 2)),
    ]
    if with_out:
        scratch += [
            pltpu.VMEM((2, D, HALF), jnp.bfloat16),
            pltpu.SemaphoreType.DMA((2,)),
            pltpu.VMEM((HALF // 128, 2048, 128), jnp.float32),
        ]
    return pl.pallas_call(
        functools.partial(layer_kernel, first_block, with_out),
        grid_spec=pltpu.PrefetchScalarGridSpec(
            num_scalar_prefetch=3,
            grid=(STEPS,),
            in_specs=[hbm] * (2 * PIECES) + whole,
            out_specs=pl.BlockSpec((BLK, D), lambda i, *s: (0, 0)),
            scratch_shapes=scratch,
        ),
        out_shape=jax.ShapeDtypeStruct((BLK, D), jnp.bfloat16),
        compiler_params=pltpu.CompilerParams(
            dimension_semantics=("arbitrary",), vmem_limit_bytes=60 * 1024 * 1024
        ),
        cost_estimate=pl.CostEstimate(
            flops=8 * 10**9, bytes_accessed=14 * 10**6, transcendentals=4 * 10**6
        ),
    )(scal, lengths, matchings, *mine, *yours, *rows)


def next_to(block):
    return lax.ppermute(block, ALL, X_DOWN), lax.ppermute(block, ALL, X_UP)


def other_core(pieces):
    return tuple(lax.ppermute(piece, ALL, CORE_SWAP) for piece in pieces)


def gather_rows(weights, width, x, core, y_hi):
    def column_block(half):
        columns = weights(half)
        return jnp.concatenate(
            [
                lax.dynamic_slice_in_dim(columns, place * width, width, 1)
                for place in (x, (x + 2) & 3)
            ],
            axis=1,
        )

    keep, give = column_block(core), column_block(1 - core)
    near = lax.ppermute(give, ALL, CORE_SWAP)
    cross = lax.ppermute(keep, ALL, CROSS_SWAP)
    far = lax.ppermute(give, ALL, FAR_SWAP)

    def in_order(mine_first, mine, yours):
        return jnp.where(
            mine_first,
            jnp.concatenate([mine, yours], axis=0),
            jnp.concatenate([yours, mine], axis=0),
        )

    return in_order(
        y_hi == 0, in_order(core == 0, keep, near), in_order(core == 0, cross, far)
    )


def local(frames, lengths, matchings, wqkv, wout):
    gx, gy = lax.axis_index("gx"), lax.axis_index("gy")
    here = gx * 32 + gy
    core, y_hi, x = gy & 1, (gy >> 1) & 1, gx >> 1

    def half_0(half):
        columns = jnp.concatenate([wqkv[0], wout[0]], axis=1).reshape(-1, 4, 2, HALF)
        return lax.dynamic_index_in_dim(columns, half, 2, keepdims=False).reshape(-1, 4 * HALF)

    plane_0 = gather_rows(half_0, WIDTHS[0], x, core, y_hi)

    spread_in = frames.reshape(2, HALO, 2, HALF).transpose(2, 1, 0, 3).reshape(256, 2, HALF)
    plane_0, spread_in, wqkv_1 = lax.optimization_barrier((plane_0, spread_in, wqkv[1]))

    def half_1(half):
        columns = wqkv_1.reshape(-1, 3, 2, HALF)
        columns = lax.dynamic_index_in_dim(columns, half, 2, keepdims=False).reshape(-1, 3 * HALF)
        return jnp.pad(columns, ((0, 0), (0, 4 * WIDTHS[1] - 3 * HALF)))

    plane_1 = gather_rows(half_1, WIDTHS[1], x, core, y_hi)
    columns_0, columns_1 = (
        lax.all_gather(part, "gy", axis=0, tiled=True, axis_index_groups=Z_GROUPS)
        for part in (plane_0, plane_1)
    )
    spread = lax.all_to_all(spread_in, ALL, 0, 0, tiled=True).reshape(512, HALF)

    partner_0, partner_1 = matchings[0], matchings[1]
    second = lookup_all(partner_0, partner_1)
    before = jnp.maximum(jnp.arange(256, dtype=jnp.int32) - 1, 0)
    before_1 = jnp.maximum(partner_1 - 1, 0)
    high = ((here & (HALO - 1)) < jnp.maximum(lengths - HALO, 0)).astype(jnp.int32)
    wanted = jnp.stack(
        [
            2 * partner_0,
            2 * partner_0 + 1,
            2 * partner_1,
            2 * partner_1 + 1,
            2 * second,
            2 * second + 1,
            2 * before_1 + lookup_all(high, before_1),
            2 * before + lookup_all(high, before),
        ],
        axis=1,
    ).reshape(-1)
    chosen = (wanted[:, None] == jnp.arange(512, dtype=jnp.int32)[None, :]).astype(jnp.bfloat16)
    routed = jnp.dot(chosen, spread, preferred_element_type=jnp.float32).astype(jnp.bfloat16)
    columns_0, _ = lax.optimization_barrier((columns_0, routed))
    collected = lax.all_to_all(routed.reshape(256, 8, HALF), ALL, 0, 0, tiled=True)
    collected = collected.reshape(2048, HALF)

    near_0 = next_to(columns_0[:, : WIDTHS[0]])
    mine_0 = (columns_0, *near_0)
    yours_0 = other_core(mine_0)
    columns_1, near_0 = lax.optimization_barrier((columns_1, near_0))
    near_1 = next_to(columns_1[:, : WIDTHS[1]])

    scal = jnp.stack([here, core, x]).astype(jnp.int32)
    run = functools.partial(layer, scal, lengths, matchings)
    hidden = run(mine_0, yours_0, (frames, collected), True, True)
    tail_start = jnp.maximum(lookup(lengths, here) - HALO, 0)
    own_tail = lax.dynamic_slice_in_dim(hidden, tail_start, HALO, 0)
    tail = lax.ppermute(own_tail, ALL, [(i, i + 1) for i in range(255)])
    far_1 = other_core((columns_1,))
    hidden_1 = run(mine_0, yours_0, (collected,), False, True)
    near_1, hidden, hidden_1 = lax.optimization_barrier((near_1, hidden, hidden_1))
    mine_1, yours_1 = (columns_1, *near_1), (*far_1, *other_core(near_1))
    context = run(mine_1, yours_1, (hidden, hidden_1, tail), True, False)
    return hidden, context


def solution(mesh):
    rows = P(ALL, None)
    return jax.shard_map(
        local,
        mesh=mesh,
        in_specs=(rows, P(), P(), P(None, "gy", None), P(None, "gy", None)),
        out_specs=(rows, rows),
        check_vma=False,
    )
```

```python
import functools
import math

import jax
import jax.numpy as jnp
from jax import lax
from jax.experimental import pallas as pl
from jax.experimental.pallas import tpu as pltpu
from jax.sharding import PartitionSpec as P

ALL = ("gx", "gy")
HEAD_DIM = 64
HALO = 128
BLK = 256
D = 1280
HALF = D // 2
PAIR = 2 * HEAD_DIM
STEPS = D // (2 * PAIR)
WIDTHS = (HALF, 512)
SCALE_LOG2 = 0.125 * math.log2(math.e)


def flat_pairs(move):
    pairs = []
    for gx in range(8):
        for gy in range(32):
            x, y_lo, z, y_hi, core = move(gx // 2, gx % 2, gy // 4, (gy // 2) % 2, gy % 2)
            pairs.append((gx * 32 + gy, (x % 4 * 2 + y_lo) * 32 + z % 8 * 4 + y_hi * 2 + core))
    return pairs


CORE_SWAP = flat_pairs(lambda x, l, z, h, c: (x, l, z, h, 1 - c))
CROSS_SWAP = flat_pairs(lambda x, l, z, h, c: (x, 1 - l, z, 1 - h, c))
FAR_SWAP = flat_pairs(lambda x, l, z, h, c: (x, 1 - l, z, 1 - h, 1 - c))
X_UP = flat_pairs(lambda x, l, z, h, c: (x + 1, l, z, h, c))
X_DOWN = flat_pairs(lambda x, l, z, h, c: (x - 1, l, z, h, c))
Z_GROUPS = [[z * 4 + k for z in range(8)] for k in range(4)]


def lookup(table, index):
    return jnp.sum(jnp.where(jnp.arange(table.shape[0], dtype=jnp.int32) == index, table, 0))


def lookup_all(table, index):
    ids = jnp.arange(table.shape[0], dtype=jnp.int32)
    return jnp.sum(jnp.where(ids[None, :] == index[:, None], table[None, :], 0), axis=1)


def standardized(rows):
    values = rows.astype(jnp.float32)
    mean = jnp.mean(values, axis=-1, keepdims=True)
    centred = values - mean
    variance = jnp.mean(centred * centred, axis=-1, keepdims=True)
    return (centred * lax.rsqrt(variance + 1e-05)).astype(jnp.bfloat16)


def layer_kernel(first_block, with_out, scal, lengths, matchings, *refs):
    width_here = WIDTHS[0 if with_out else 1]
    tiles = width_here // PAIR
    pieces = 3 if with_out else 5
    sources, refs = (refs[:pieces], refs[pieces : 2 * pieces]), refs[2 * pieces :]
    if first_block:
        own, refs = refs[0], refs[1:]
    if with_out:
        collected, out, normed, ctx, weights, weight_sems, out_weights, out_sems, spare = refs
    else:
        other, tail, out, normed, ctx, weights, weight_sems = refs
    step = pl.program_id(0)
    here, core, x = scal[0], scal[1], scal[2]
    block = here if first_block else matchings[1, here]
    partner = matchings[0 if with_out else 1, block]
    known = jnp.minimum(lengths[jnp.maximum(block - 1, 0)], HALO)
    known = jnp.where(block > 0, known, 0)

    def slot_half(at, half):
        rows = pl.ds(half * 1024 + at, HALO, stride=8)
        return jnp.concatenate([spare[i, rows, :] for i in range(HALF // 128)], axis=1)

    def start_tile(half, x_here, index, target, width, sem):
        place = (index // tiles - x_here) % 4
        column = index % tiles * PAIR
        side, columns = sources[half], pl.ds(column, width)
        if place == 2 and with_out:
            copies = [(side[0].at[:, pl.ds(width_here + column, width)], target)]
        elif place == 2:
            copies = [
                (side[3 + part].at[:, columns], target.at[pl.ds(part * (D // 2), D // 2)])
                for part in range(2)
            ]
        else:
            copies = [(side[(0, 1, None, 2)[place]].at[:, columns], target)]
        for source, piece in copies:
            pltpu.make_async_copy(source, piece, sem).start()

    @pl.when(step == 0)
    def _():
        for x_here in range(4):

            @pl.when(x == x_here)
            def _():
                for at in range(STEPS):
                    for kind in range(3):
                        for half in range(2):
                            start_tile(
                                half,
                                x_here,
                                kind * STEPS + at,
                                weights.at[at, kind, :, pl.ds(half * PAIR, PAIR)],
                                PAIR,
                                weight_sems.at[at, kind, half],
                            )
                if with_out:
                    for half in range(2):
                        start_tile(
                            half, x_here, 3 * STEPS, out_weights.at[half], HALF, out_sems.at[half]
                        )

        if with_out:
            for lane_tile in range(HALF // 128):
                lanes = pl.ds(lane_tile * 128, 128)
                spare[lane_tile] = collected[:, lanes].astype(jnp.float32)

            def slot(at):
                return jnp.concatenate([slot_half(at, 0), slot_half(at, 1)], axis=1)

            slots = (0, 1, 7) if first_block else (2, 3, 4, 5, 6)
            if first_block:
                normed[pl.ds(0, BLK), :] = standardized(own[...])
            base = BLK if first_block else 0
            for order, at in enumerate(slots):
                normed[pl.ds(base + order * HALO, HALO), :] = standardized(slot(at))
        else:
            normed[pl.ds(0, BLK), :] = standardized(own[...])
            normed[pl.ds(BLK, BLK), :] = standardized(other[...])
            normed[pl.ds(2 * BLK, HALO), :] = standardized(tail[...])

    for kind in range(3):
        for half in range(2):
            target = weights.at[step, kind, :, pl.ds(half * PAIR, PAIR)]
            pltpu.make_async_copy(target, target, weight_sems.at[step, kind, half]).wait()

    count = 2 * BLK + HALO
    row = lax.broadcasted_iota(jnp.int32, (count, PAIR), 0)
    lane_k = lax.broadcasted_iota(jnp.int32, (count, PAIR), 1)
    lane_q = lax.broadcasted_iota(jnp.int32, (BLK, PAIR), 1)
    limit = jnp.where(
        row < BLK,
        lengths[block],
        jnp.where(row < 2 * BLK, lengths[partner] + BLK, known + 2 * BLK),
    )
    bias = jnp.where(row < limit, 0.0, -1e30).astype(jnp.float32)

    x_all = normed[...]
    dot = functools.partial(jnp.dot, preferred_element_type=jnp.float32)
    q = dot(normed[pl.ds(0, BLK), :], weights[step, 0])
    k = dot(x_all, weights[step, 1])
    v = dot(x_all, weights[step, 2]).astype(jnp.bfloat16)
    for pair in range(2):
        lanes = slice(pair * PAIR, (pair + 1) * PAIR)
        q_pair, k_pair, v_pair = q[:, lanes], k[:, lanes], v[:, lanes]
        parts = []
        for head in range(2):
            mine_q = (lane_q < HEAD_DIM) if head == 0 else (lane_q >= HEAD_DIM)
            free = HEAD_DIM if head == 0 else 0
            q_head = jnp.where(
                mine_q, q_pair, jnp.where(lane_q == free, 1.0, 0.0)
            ).astype(jnp.bfloat16)
            k_head = jnp.where(lane_k == free, bias, k_pair).astype(jnp.bfloat16)
            scores = lax.dot_general(
                q_head, k_head, (((1,), (1,)), ((), ())), preferred_element_type=jnp.float32
            )
            top = jnp.max(scores, axis=-1, keepdims=True)
            expo = jnp.exp2((scores - top) * SCALE_LOG2)
            total = jnp.sum(expo, axis=-1, keepdims=True)
            mixed = dot(expo.astype(jnp.bfloat16), v_pair)
            parts.append(mixed / total)
        both = jnp.where(lane_q < HEAD_DIM, parts[0], parts[1]).astype(jnp.bfloat16)
        half = core if pair == 0 else 1 - core
        place = pl.multiple_of((half * STEPS + step) * PAIR, PAIR)
        ctx[:, pl.ds(place, PAIR)] = both

    @pl.when(step == STEPS - 1)
    def _():
        if with_out:
            context = ctx[...]
            for half in range(2):
                target = out_weights.at[half]
                pltpu.make_async_copy(target, target, out_sems.at[half]).wait()
                update = dot(context, target[...])
                absolute = core if half == 0 else 1 - core
                if first_block:
                    place = pl.ds(pl.multiple_of(absolute * HALF, 128), HALF)
                    here_rows = own[:, place].astype(jnp.float32)
                    out[:, place] = (here_rows + update).astype(jnp.bfloat16)
                else:
                    place = pl.ds(pl.multiple_of(absolute * HALF, 128), HALF)
                    for part in range(2):
                        rows = pl.ds(part * HALO, HALO)
                        change = update[part * HALO : (part + 1) * HALO]
                        out[rows, place] = (slot_half(2 + part, absolute) + change).astype(
                            jnp.bfloat16
                        )
        else:
            out[...] = ctx[...]


def layer(scal, lengths, matchings, mine, yours, rows, first_block, with_out):
    hbm = pl.BlockSpec(memory_space=pl.ANY)
    whole = [pl.BlockSpec(r.shape, lambda i, *s: (0, 0)) for r in rows]
    scratch = [
        pltpu.VMEM((2 * BLK + HALO, D), jnp.bfloat16),
        pltpu.VMEM((BLK, D), jnp.bfloat16),
        pltpu.VMEM((STEPS, 3, D, 2 * PAIR), jnp.bfloat16),
        pltpu.SemaphoreType.DMA((STEPS, 3, 2)),
    ]
    if with_out:
        scratch += [
            pltpu.VMEM((2, D, HALF), jnp.bfloat16),
            pltpu.SemaphoreType.DMA((2,)),
            pltpu.VMEM((HALF // 128, 2048, 128), jnp.float32),
        ]
    return pl.pallas_call(
        functools.partial(layer_kernel, first_block, with_out),
        grid_spec=pltpu.PrefetchScalarGridSpec(
            num_scalar_prefetch=3,
            grid=(STEPS,),
            in_specs=[hbm] * (len(mine) + len(yours)) + whole,
            out_specs=pl.BlockSpec((BLK, D), lambda i, *s: (0, 0)),
            scratch_shapes=scratch,
        ),
        out_shape=jax.ShapeDtypeStruct((BLK, D), jnp.bfloat16),
        compiler_params=pltpu.CompilerParams(
            dimension_semantics=("arbitrary",), vmem_limit_bytes=60 * 1024 * 1024
        ),
        cost_estimate=pl.CostEstimate(
            flops=8 * 10**9, bytes_accessed=14 * 10**6, transcendentals=4 * 10**6
        ),
    )(scal, lengths, matchings, *mine, *yours, *rows)


def next_to(block):
    return lax.ppermute(block, ALL, X_DOWN), lax.ppermute(block, ALL, X_UP)


def other_core(pieces):
    return tuple(lax.ppermute(piece, ALL, CORE_SWAP) for piece in pieces)


def gather_rows(weights, width, places, core, y_hi):
    def column_block(half):
        columns = weights(half)
        return jnp.concatenate(
            [
                lax.dynamic_slice_in_dim(columns, place * width, width, 1)
                for place in places
            ],
            axis=1,
        )

    keep, give = column_block(core), column_block(1 - core)
    near = lax.ppermute(give, ALL, CORE_SWAP)
    cross = lax.ppermute(keep, ALL, CROSS_SWAP)
    far = lax.ppermute(give, ALL, FAR_SWAP)

    def in_order(mine_first, mine, yours):
        return jnp.where(
            mine_first,
            jnp.concatenate([mine, yours], axis=0),
            jnp.concatenate([yours, mine], axis=0),
        )

    return in_order(
        y_hi == 0, in_order(core == 0, keep, near), in_order(core == 0, cross, far)
    )


def local(frames, lengths, matchings, wqkv, wout):
    gx, gy = lax.axis_index("gx"), lax.axis_index("gy")
    here = gx * 32 + gy
    core, y_hi, x = gy & 1, (gy >> 1) & 1, gx >> 1

    def half_0(half):
        columns = jnp.concatenate([wqkv[0], wout[0]], axis=1).reshape(-1, 4, 2, HALF)
        return lax.dynamic_index_in_dim(columns, half, 2, keepdims=False).reshape(-1, 4 * HALF)

    plane_0 = gather_rows(half_0, WIDTHS[0], (x, (x + 2) & 3), core, y_hi)

    spread_in = frames.reshape(2, HALO, 2, HALF).transpose(2, 1, 0, 3).reshape(256, 2, HALF)
    plane_0, spread_in, wqkv_1 = lax.optimization_barrier((plane_0, spread_in, wqkv[1]))

    def half_1(half):
        columns = wqkv_1.reshape(-1, 3, 2, HALF)
        columns = lax.dynamic_index_in_dim(columns, half, 2, keepdims=False).reshape(-1, 3 * HALF)
        return jnp.pad(columns, ((0, 0), (0, 4 * WIDTHS[1] - 3 * HALF)))

    plane_1 = gather_rows(half_1, WIDTHS[1], (x,), core, y_hi)
    columns_0, columns_1 = (
        lax.all_gather(part, "gy", axis=0, tiled=True, axis_index_groups=Z_GROUPS)
        for part in (plane_0, plane_1)
    )
    spread = lax.all_to_all(spread_in, ALL, 0, 0, tiled=True).reshape(512, HALF)

    partner_0, partner_1 = matchings[0], matchings[1]
    second = lookup_all(partner_0, partner_1)
    before = jnp.maximum(jnp.arange(256, dtype=jnp.int32) - 1, 0)
    before_1 = jnp.maximum(partner_1 - 1, 0)
    high = ((here & (HALO - 1)) < jnp.maximum(lengths - HALO, 0)).astype(jnp.int32)
    wanted = jnp.stack(
        [
            2 * partner_0,
            2 * partner_0 + 1,
            2 * partner_1,
            2 * partner_1 + 1,
            2 * second,
            2 * second + 1,
            2 * before_1 + lookup_all(high, before_1),
            2 * before + lookup_all(high, before),
        ],
        axis=1,
    ).reshape(-1)
    chosen = (wanted[:, None] == jnp.arange(512, dtype=jnp.int32)[None, :]).astype(jnp.bfloat16)
    spread, _ = lax.optimization_barrier((spread, plane_1))
    routed = jnp.dot(chosen, spread, preferred_element_type=jnp.float32).astype(jnp.bfloat16)
    columns_0, _ = lax.optimization_barrier((columns_0, routed))
    collected = lax.all_to_all(routed.reshape(256, 8, HALF), ALL, 0, 0, tiled=True)
    collected = collected.reshape(2048, HALF)

    near_0 = next_to(columns_0[:, : WIDTHS[0]])
    mine_0 = (columns_0, *near_0)
    yours_0 = other_core(mine_0)
    columns_1, near_0 = lax.optimization_barrier((columns_1, near_0))
    near_1 = next_to(columns_1)

    scal = jnp.stack([here, core, x]).astype(jnp.int32)
    run = functools.partial(layer, scal, lengths, matchings)
    hidden = run(mine_0, yours_0, (frames, collected), True, True)
    tail_start = jnp.maximum(lookup(lengths, here) - HALO, 0)
    own_tail = lax.dynamic_slice_in_dim(hidden, tail_start, HALO, 0)
    tail = lax.ppermute(own_tail, ALL, [(i, i + 1) for i in range(255)])
    here_1 = other_core((columns_1,))
    hidden_1 = run(mine_0, yours_0, (collected,), False, True)
    near_1, hidden_1 = lax.optimization_barrier((near_1, hidden_1))
    above, below = near_1
    far_1 = (
        lax.ppermute(below[: D // 2], ALL, X_UP),
        lax.ppermute(above[D // 2 :], ALL, X_DOWN),
    )
    near_swapped = other_core(near_1)
    far_1, hidden, hidden_1 = lax.optimization_barrier((far_1, hidden, hidden_1))
    mine_1 = (columns_1, *near_1, *far_1)
    yours_1 = (*here_1, *near_swapped, *other_core(far_1))
    context = run(mine_1, yours_1, (hidden, hidden_1, tail), True, False)
    return hidden, context


def solution(mesh):
    rows = P(ALL, None)
    return jax.shard_map(
        local,
        mesh=mesh,
        in_specs=(rows, P(), P(), P(None, "gy", None), P(None, "gy", None)),
        out_specs=(rows, rows),
        check_vma=False,
    )
```

```python
import functools
import math

import jax
import jax.numpy as jnp
from jax import lax
from jax.experimental import pallas as pl
from jax.experimental.pallas import tpu as pltpu
from jax.sharding import PartitionSpec as P

ALL = ("gx", "gy")
HEAD_DIM = 64
HALO = 128
BLK = 256
D = 1280
HALF = D // 2
PAIR = 2 * HEAD_DIM
STEPS = D // (2 * PAIR)
WIDTHS = (HALF, 512)
SCALE_LOG2 = 0.125 * math.log2(math.e)


def flat_pairs(move):
    pairs = []
    for gx in range(8):
        for gy in range(32):
            x, y_lo, z, y_hi, core = move(gx // 2, gx % 2, gy // 4, (gy // 2) % 2, gy % 2)
            pairs.append((gx * 32 + gy, (x % 4 * 2 + y_lo) * 32 + z % 8 * 4 + y_hi * 2 + core))
    return pairs


CORE_SWAP = flat_pairs(lambda x, l, z, h, c: (x, l, z, h, 1 - c))
CROSS_SWAP = flat_pairs(lambda x, l, z, h, c: (x, 1 - l, z, 1 - h, c))
FAR_SWAP = flat_pairs(lambda x, l, z, h, c: (x, 1 - l, z, 1 - h, 1 - c))
X_UP = flat_pairs(lambda x, l, z, h, c: (x + 1, l, z, h, c))
X_DOWN = flat_pairs(lambda x, l, z, h, c: (x - 1, l, z, h, c))
Z_GROUPS = [[z * 4 + k for z in range(8)] for k in range(4)]


def lookup(table, index):
    return jnp.sum(jnp.where(jnp.arange(table.shape[0], dtype=jnp.int32) == index, table, 0))


def lookup_all(table, index):
    ids = jnp.arange(table.shape[0], dtype=jnp.int32)
    return jnp.sum(jnp.where(ids[None, :] == index[:, None], table[None, :], 0), axis=1)


def standardized(rows):
    values = rows.astype(jnp.float32)
    mean = jnp.mean(values, axis=-1, keepdims=True)
    centred = values - mean
    variance = jnp.mean(centred * centred, axis=-1, keepdims=True)
    return (centred * lax.rsqrt(variance + 1e-05)).astype(jnp.bfloat16)


def layer_kernel(first_block, with_out, scal, lengths, matchings, *refs):
    width_here = WIDTHS[0 if with_out else 1]
    tiles = width_here // PAIR
    pieces = 3 if with_out else 4
    sources, refs = (refs[:pieces], refs[pieces : 2 * pieces]), refs[2 * pieces :]
    if first_block:
        own, refs = refs[0], refs[1:]
    if with_out:
        collected, out, normed, ctx, weights, weight_sems, out_weights, out_sems, spare = refs
    else:
        other, tail, out, normed, ctx, weights, weight_sems = refs
    step = pl.program_id(0)
    here, core, x = scal[0], scal[1], scal[2]
    block = here if first_block else matchings[1, here]
    partner = matchings[0 if with_out else 1, block]
    known = jnp.minimum(lengths[jnp.maximum(block - 1, 0)], HALO)
    known = jnp.where(block > 0, known, 0)

    def slot_half(at, half):
        rows = pl.ds(half * 1024 + at, HALO, stride=8)
        return jnp.concatenate([spare[i, rows, :] for i in range(HALF // 128)], axis=1)

    def start_tile(half, x_here, index, target, width, sem):
        place = (index // tiles - x_here) % 4
        column = index % tiles * PAIR
        if not with_out:
            piece = place
        elif place % 2 == 0:
            piece = 0
            column += place // 2 * width_here
        else:
            piece = 1 + place // 2
        source = sources[half][piece].at[:, pl.ds(column, width)]
        pltpu.make_async_copy(source, target, sem).start()

    @pl.when(step == 0)
    def _():
        for x_here in range(4):

            @pl.when(x == x_here)
            def _():
                for at in range(STEPS):
                    for kind in range(3):
                        for half in range(2):
                            start_tile(
                                half,
                                x_here,
                                kind * STEPS + at,
                                weights.at[at, kind, :, pl.ds(half * PAIR, PAIR)],
                                PAIR,
                                weight_sems.at[at, kind, half],
                            )
                if with_out:
                    for half in range(2):
                        start_tile(
                            half, x_here, 3 * STEPS, out_weights.at[half], HALF, out_sems.at[half]
                        )

        if with_out:
            for lane_tile in range(HALF // 128):
                lanes = pl.ds(lane_tile * 128, 128)
                spare[lane_tile] = collected[:, lanes].astype(jnp.float32)

            def slot(at):
                return jnp.concatenate([slot_half(at, 0), slot_half(at, 1)], axis=1)

            slots = (0, 1, 7) if first_block else (2, 3, 4, 5, 6)
            if first_block:
                normed[pl.ds(0, BLK), :] = standardized(own[...])
            base = BLK if first_block else 0
            for order, at in enumerate(slots):
                normed[pl.ds(base + order * HALO, HALO), :] = standardized(slot(at))
        else:
            normed[pl.ds(0, BLK), :] = standardized(own[...])
            normed[pl.ds(BLK, BLK), :] = standardized(other[...])
            normed[pl.ds(2 * BLK, HALO), :] = standardized(tail[...])

    for kind in range(3):
        for half in range(2):
            target = weights.at[step, kind, :, pl.ds(half * PAIR, PAIR)]
            pltpu.make_async_copy(target, target, weight_sems.at[step, kind, half]).wait()

    count = 2 * BLK + HALO
    row = lax.broadcasted_iota(jnp.int32, (count, PAIR), 0)
    lane_k = lax.broadcasted_iota(jnp.int32, (count, PAIR), 1)
    lane_q = lax.broadcasted_iota(jnp.int32, (BLK, PAIR), 1)
    limit = jnp.where(
        row < BLK,
        lengths[block],
        jnp.where(row < 2 * BLK, lengths[partner] + BLK, known + 2 * BLK),
    )
    bias = jnp.where(row < limit, 0.0, -1e30).astype(jnp.float32)

    x_all = normed[...]
    dot = functools.partial(jnp.dot, preferred_element_type=jnp.float32)
    q = dot(normed[pl.ds(0, BLK), :], weights[step, 0])
    k = dot(x_all, weights[step, 1])
    v = dot(x_all, weights[step, 2]).astype(jnp.bfloat16)
    for pair in range(2):
        lanes = slice(pair * PAIR, (pair + 1) * PAIR)
        q_pair, k_pair, v_pair = q[:, lanes], k[:, lanes], v[:, lanes]
        parts = []
        for head in range(2):
            mine_q = (lane_q < HEAD_DIM) if head == 0 else (lane_q >= HEAD_DIM)
            free = HEAD_DIM if head == 0 else 0
            q_head = jnp.where(
                mine_q, q_pair, jnp.where(lane_q == free, 1.0, 0.0)
            ).astype(jnp.bfloat16)
            k_head = jnp.where(lane_k == free, bias, k_pair).astype(jnp.bfloat16)
            scores = lax.dot_general(
                q_head, k_head, (((1,), (1,)), ((), ())), preferred_element_type=jnp.float32
            )
            top = jnp.max(scores, axis=-1, keepdims=True)
            expo = jnp.exp2((scores - top) * SCALE_LOG2)
            total = jnp.sum(expo, axis=-1, keepdims=True)
            mixed = dot(expo.astype(jnp.bfloat16), v_pair)
            parts.append(mixed / total)
        both = jnp.where(lane_q < HEAD_DIM, parts[0], parts[1]).astype(jnp.bfloat16)
        half = core if pair == 0 else 1 - core
        place = pl.multiple_of((half * STEPS + step) * PAIR, PAIR)
        ctx[:, pl.ds(place, PAIR)] = both

    @pl.when(step == STEPS - 1)
    def _():
        if with_out:
            context = ctx[...]
            for half in range(2):
                target = out_weights.at[half]
                pltpu.make_async_copy(target, target, out_sems.at[half]).wait()
                update = dot(context, target[...])
                absolute = core if half == 0 else 1 - core
                if first_block:
                    place = pl.ds(pl.multiple_of(absolute * HALF, 128), HALF)
                    here_rows = own[:, place].astype(jnp.float32)
                    out[:, place] = (here_rows + update).astype(jnp.bfloat16)
                else:
                    place = pl.ds(pl.multiple_of(absolute * HALF, 128), HALF)
                    for part in range(2):
                        rows = pl.ds(part * HALO, HALO)
                        change = update[part * HALO : (part + 1) * HALO]
                        out[rows, place] = (slot_half(2 + part, absolute) + change).astype(
                            jnp.bfloat16
                        )
        else:
            out[...] = ctx[...]


def layer(scal, lengths, matchings, mine, yours, rows, first_block, with_out):
    hbm = pl.BlockSpec(memory_space=pl.ANY)
    whole = [pl.BlockSpec(r.shape, lambda i, *s: (0, 0)) for r in rows]
    scratch = [
        pltpu.VMEM((2 * BLK + HALO, D), jnp.bfloat16),
        pltpu.VMEM((BLK, D), jnp.bfloat16),
        pltpu.VMEM((STEPS, 3, D, 2 * PAIR), jnp.bfloat16),
        pltpu.SemaphoreType.DMA((STEPS, 3, 2)),
    ]
    if with_out:
        scratch += [
            pltpu.VMEM((2, D, HALF), jnp.bfloat16),
            pltpu.SemaphoreType.DMA((2,)),
            pltpu.VMEM((HALF // 128, 2048, 128), jnp.float32),
        ]
    return pl.pallas_call(
        functools.partial(layer_kernel, first_block, with_out),
        grid_spec=pltpu.PrefetchScalarGridSpec(
            num_scalar_prefetch=3,
            grid=(STEPS,),
            in_specs=[hbm] * (len(mine) + len(yours)) + whole,
            out_specs=pl.BlockSpec((BLK, D), lambda i, *s: (0, 0)),
            scratch_shapes=scratch,
        ),
        out_shape=jax.ShapeDtypeStruct((BLK, D), jnp.bfloat16),
        compiler_params=pltpu.CompilerParams(
            dimension_semantics=("arbitrary",), vmem_limit_bytes=60 * 1024 * 1024
        ),
        cost_estimate=pl.CostEstimate(
            flops=8 * 10**9, bytes_accessed=14 * 10**6, transcendentals=4 * 10**6
        ),
    )(scal, lengths, matchings, *mine, *yours, *rows)


def next_to(block):
    return lax.ppermute(block, ALL, X_DOWN), lax.ppermute(block, ALL, X_UP)


def other_core(pieces):
    return tuple(lax.ppermute(piece, ALL, CORE_SWAP) for piece in pieces)


def gather_rows(weights, width, x, core, y_hi):
    def column_block(half):
        columns = weights(half)
        return jnp.concatenate(
            [
                lax.dynamic_slice_in_dim(columns, place * width, width, 1)
                for place in (x, (x + 2) & 3)
            ],
            axis=1,
        )

    keep, give = column_block(core), column_block(1 - core)
    near = lax.ppermute(give, ALL, CORE_SWAP)
    cross = lax.ppermute(keep, ALL, CROSS_SWAP)
    far = lax.ppermute(give, ALL, FAR_SWAP)

    def in_order(mine_first, mine, yours):
        return jnp.where(
            mine_first,
            jnp.concatenate([mine, yours], axis=0),
            jnp.concatenate([yours, mine], axis=0),
        )

    return in_order(
        y_hi == 0, in_order(core == 0, keep, near), in_order(core == 0, cross, far)
    )


def local(frames, lengths, matchings, wqkv, wout):
    gx, gy = lax.axis_index("gx"), lax.axis_index("gy")
    here = gx * 32 + gy
    core, y_hi, x = gy & 1, (gy >> 1) & 1, gx >> 1

    def half_0(half):
        columns = jnp.concatenate([wqkv[0], wout[0]], axis=1).reshape(-1, 4, 2, HALF)
        return lax.dynamic_index_in_dim(columns, half, 2, keepdims=False).reshape(-1, 4 * HALF)

    plane_0 = gather_rows(half_0, WIDTHS[0], x, core, y_hi)

    spread_in = frames.reshape(2, HALO, 2, HALF).transpose(2, 1, 0, 3).reshape(256, 2, HALF)
    plane_0, spread_in, wqkv_1 = lax.optimization_barrier((plane_0, spread_in, wqkv[1]))

    def half_1(half):
        columns = wqkv_1.reshape(-1, 3, 2, HALF)
        columns = lax.dynamic_index_in_dim(columns, half, 2, keepdims=False).reshape(-1, 3 * HALF)
        return jnp.pad(columns, ((0, 0), (0, 4 * WIDTHS[1] - 3 * HALF)))

    plane_1 = gather_rows(half_1, WIDTHS[1], x, core, y_hi)
    columns_0, columns_1, far_1 = (
        lax.all_gather(part, "gy", axis=0, tiled=True, axis_index_groups=Z_GROUPS)
        for part in (plane_0, plane_1[:, : WIDTHS[1]], plane_1[:, WIDTHS[1] :])
    )
    spread = lax.all_to_all(spread_in, ALL, 0, 0, tiled=True).reshape(512, HALF)

    partner_0, partner_1 = matchings[0], matchings[1]
    second = lookup_all(partner_0, partner_1)
    before = jnp.maximum(jnp.arange(256, dtype=jnp.int32) - 1, 0)
    before_1 = jnp.maximum(partner_1 - 1, 0)
    high = ((here & (HALO - 1)) < jnp.maximum(lengths - HALO, 0)).astype(jnp.int32)
    wanted = jnp.stack(
        [
            2 * partner_0,
            2 * partner_0 + 1,
            2 * partner_1,
            2 * partner_1 + 1,
            2 * second,
            2 * second + 1,
            2 * before_1 + lookup_all(high, before_1),
            2 * before + lookup_all(high, before),
        ],
        axis=1,
    ).reshape(-1)
    chosen = (wanted[:, None] == jnp.arange(512, dtype=jnp.int32)[None, :]).astype(jnp.bfloat16)
    spread, _ = lax.optimization_barrier((spread, plane_1))
    routed = jnp.dot(chosen, spread, preferred_element_type=jnp.float32).astype(jnp.bfloat16)
    columns_0, _ = lax.optimization_barrier((columns_0, routed))
    collected = lax.all_to_all(routed.reshape(256, 8, HALF), ALL, 0, 0, tiled=True)
    collected = collected.reshape(2048, HALF)

    near_0 = next_to(columns_0[:, : WIDTHS[0]])
    mine_0 = (columns_0, *near_0)
    yours_0 = other_core(mine_0)
    columns_1, near_0 = lax.optimization_barrier((columns_1, near_0))
    near_1 = next_to(columns_1)

    scal = jnp.stack([here, core, x]).astype(jnp.int32)
    run = functools.partial(layer, scal, lengths, matchings)
    hidden = run(mine_0, yours_0, (frames, collected), True, True)
    tail_start = jnp.maximum(lookup(lengths, here) - HALO, 0)
    own_tail = lax.dynamic_slice_in_dim(hidden, tail_start, HALO, 0)
    tail = lax.ppermute(own_tail, ALL, [(i, i + 1) for i in range(255)])
    here_1 = other_core((columns_1,))
    hidden_1 = run(mine_0, yours_0, (collected,), False, True)
    near_1, far_1, hidden, hidden_1 = lax.optimization_barrier((near_1, far_1, hidden, hidden_1))
    mine_1 = (columns_1, near_1[0], far_1, near_1[1])
    yours_1 = (*here_1, *other_core(mine_1[1:]))
    context = run(mine_1, yours_1, (hidden, hidden_1, tail), True, False)
    return hidden, context


def solution(mesh):
    rows = P(ALL, None)
    return jax.shard_map(
        local,
        mesh=mesh,
        in_specs=(rows, P(), P(), P(None, "gy", None), P(None, "gy", None)),
        out_specs=(rows, rows),
        check_vma=False,
    )
```
